128 devices in a mesh: layer: 4 (over x), energy: 32 (over y, z, core).
Axes of the slice: x: 4, y: 4, z: 4, core: 2. Of those that a mesh axis runs over, the one named last changes fastest.
Arguments:
- onsite: float32 [4, 256], P('layer'), may hold values from -1 to 1
- broadening: float32 [4, 256], P('layer'), may hold values from 1 to 2
- hamiltonian: float32 [4, 2, 256, 256], P('layer'), may hold values from -0.078125 to 0.078125
- coupling: float32 [4, 2, 256, 256], P('layer'), may hold values from -0.21875 to 0.21875
- coupling_mask: int32 [4, 256, 256], P('layer'), may hold values 0 or 1
- prior_sigma: float32 [4, 128, 2, 256, 256], P('layer', 'energy'), may hold values from -0.4 to 0.4, as said below
- kernel_weights: float32 [8], replicated, may hold values from 0.1 to 0.6
- kernel_offsets: int32 [8], replicated, may hold values from -7 to 7
Outputs:
- self_energy: float32 [4, 128, 2, 256, 256], P('layer', 'energy')
The draws below stay inside these ranges and needn't reach their ends.
Inputs may be any that keep to these rules, and one draw needn't show every extreme that they name: `prior_sigma`: real and imaginary parts of the blocks.
All inputs are finite; a program needn't handle non-finite values. No bound on the sum of `coupling_mask` on one device may be relied on, other than what follows from the above.
Results may differ from the reference program's by a relative error of at most 0.0001.
Values sent between devices are 32-bit elements; how exact they have to be, the bound alone decides.
A program may use at most 128 MiB of HBM per device.

```python
import math
import jax
import jax.numpy as jnp
from jax import lax

M = 256
NS_ITERS = 3
TAPS = 8
ENERGIES = 128
REACH = 7
N_LAYER = 4


def draw_prior_sigma(key, part):
    key_off, key_diag = jax.random.split(jax.random.fold_in(key, 11))
    full_shape = (N_LAYER, ENERGIES, 2, M, M)
    diag_shape = (N_LAYER, ENERGIES, 2, M)
    spread = jax.random.truncated_normal(key_off, -4.0, 4.0, full_shape, jnp.float32) * (0.1 / math.sqrt(M))
    local = jax.random.truncated_normal(key_diag, -4.0, 4.0, diag_shape, jnp.float32) * 0.1
    identity = jnp.eye(M, dtype=jnp.float32)
    return spread * (1.0 - identity) + local[..., None] * identity


def place_ends(result, stream_key, least, largest):
    longest = result.shape.index(max(result.shape))
    spots = []
    for shift in (0, 1):
        where = [jax.random.randint(jax.random.fold_in(stream_key, axis), (), 0, length) for axis, length in enumerate(result.shape)]
        where[longest] = (where[longest] + shift) % result.shape[longest]
        spots.append(tuple(where))
    return result.at[spots[0]].set(least).at[spots[1]].set(largest)


def level_of(rng, extent, cuts, low, high):
    gain = 1.0
    for axis_at, shards_of in cuts:
        heights = jax.random.uniform(jax.random.fold_in(jax.random.fold_in(rng, 6), axis_at), (shards_of,), jnp.float32, low / len(cuts), high / len(cuts))
        gain = gain * jnp.repeat(jnp.exp(heights), extent[axis_at] // shards_of).reshape((-1,) + (1,) * (len(extent) - 1 - axis_at))
    return gain


def scatter_about(own_key, dims, scale, limit, pieces=(), kind=jnp.bfloat16):
    drawn = jax.random.normal(own_key, dims, jnp.float32) * scale
    if len(pieces) > 0:
        drawn = level_of(own_key, dims, pieces, -0.22, 0.18) * drawn
    return jnp.clip(drawn, min=-limit, max=limit).astype(kind)


def setup_inputs(seed: int = 0) -> dict:
    arg_keys = jax.random.split(jax.random.key(seed), 9)
    onsite = jnp.clip(jax.random.uniform(arg_keys[0], (N_LAYER, M), jnp.float32, -1.0, 1.0) * level_of(arg_keys[0], (N_LAYER, M), ((0, 4),), -0.4, 0.0), -1.0, 1.0)
    broadening = jnp.clip(jnp.exp(math.log(2.0) - 0.6931472 * jax.random.uniform(arg_keys[1], (N_LAYER, M), jnp.float32) ** level_of(arg_keys[1], (N_LAYER, M), ((0, 4),), -0.2, 0.2)), 1.0, 2.0)
    hamiltonian = scatter_about(arg_keys[2], (N_LAYER, 2, M, M), (25 * M) ** -0.5, 0.078125, ((0, 4),), jnp.float32)
    coupling = scatter_about(arg_keys[3], (N_LAYER, 2, M, M), (3 * M) ** -0.5, 0.21875, ((0, 4),), jnp.float32)
    coupling_mask = place_ends((jax.random.randint(arg_keys[4], (N_LAYER, M, M), 0, 2) < 1).astype(jnp.int32), jax.random.fold_in(arg_keys[4], 1), 0, 1)
    prior_sigma = draw_prior_sigma(jax.random.fold_in(arg_keys[8], 71), 0)
    kernel_weights = jnp.clip(jax.random.uniform(arg_keys[6], (TAPS,), jnp.float32, 0.1, 0.6), 0.1, 0.6)
    kernel_offsets = place_ends(jax.random.randint(arg_keys[7], (TAPS,), 0 - REACH, REACH + 1), jax.random.fold_in(arg_keys[7], 1), 0 - REACH, REACH).astype(jnp.int32)
    return dict(onsite=onsite, broadening=broadening, hamiltonian=hamiltonian, coupling=coupling, coupling_mask=coupling_mask, prior_sigma=prior_sigma, kernel_weights=kernel_weights, kernel_offsets=kernel_offsets)


exact_mode = lax.Precision.HIGHEST


def matmul_high(first_op, second_op):
    return jnp.matmul(first_op, second_op, precision=exact_mode)


def complex_product(first_op, second_op):
    first_real = first_op[..., 0, :, :]
    first_imag = first_op[..., 1, :, :]
    second_real = second_op[..., 0, :, :]
    second_imag = second_op[..., 1, :, :]
    real_part = matmul_high(first_real, second_real) - matmul_high(first_imag, second_imag)
    imag_part = matmul_high(first_real, second_imag) + matmul_high(first_imag, second_real)
    return jnp.stack([real_part, imag_part], axis=-3)


def adjoint(matrix):
    return jnp.stack([jnp.swapaxes(matrix[..., 0, :, :], -1, -2), -jnp.swapaxes(matrix[..., 1, :, :], -1, -2)], axis=-3)


def lead_block(batch_size, orbitals):
    identity = jnp.eye(orbitals, dtype=jnp.float32)
    single = jnp.stack([jnp.zeros_like(identity), -0.5 * identity])
    return jnp.broadcast_to(single, (batch_size, 2, orbitals, orbitals))


def energy_levels(positions, grid_size):
    return -1.0 + 2.0 * (positions.astype(jnp.float32) + 0.5) / grid_size


def solve_layer(levels, onsite_row, damping_row, hamilton, coupler, pattern, previous, incoming, sweeps):
    orbitals = hamilton.shape[-1]
    identity = jnp.eye(orbitals, dtype=jnp.float32)
    hermitian = 0.5 * (hamilton + adjoint(hamilton))
    masked = coupler * pattern.astype(jnp.float32)[None]
    contact = complex_product(complex_product(masked[None], incoming), adjoint(masked)[None])
    real_diag = levels[:, None] - onsite_row[None, :]
    imag_diag = jnp.broadcast_to(damping_row[None, :], real_diag.shape)
    shifted = jnp.stack([real_diag, imag_diag], axis=1)[..., None, :] * identity
    system = shifted - hermitian[None] - contact - previous
    diag_real = jnp.diagonal(system[:, 0], axis1=-2, axis2=-1)
    diag_imag = jnp.diagonal(system[:, 1], axis1=-2, axis2=-1)
    modulus = diag_real * diag_real + diag_imag * diag_imag
    inverse = jnp.stack([diag_real / modulus, -diag_imag / modulus], axis=1)[..., None, :] * identity
    for sweep_no in range(sweeps):
        residue = complex_product(system, inverse)
        inverse = 2.0 * inverse - complex_product(inverse, residue)
    return inverse


def convolution_matrix(weights, offsets, row_count, col_count, margin):
    row_idx = jnp.arange(row_count, dtype=jnp.int32)
    col_idx = jnp.arange(col_count, dtype=jnp.int32)
    matches = col_idx[None, None, :] == row_idx[None, :, None] + margin + offsets[:, None, None]
    return jnp.sum(jnp.where(matches, weights[:, None, None], jnp.float32(0.0)), axis=0)


def reference(onsite, broadening, hamiltonian, coupling, coupling_mask, prior_sigma, kernel_weights, kernel_offsets):
    levels = energy_levels(jnp.arange(ENERGIES, dtype=jnp.int32), ENERGIES)
    incoming = lead_block(ENERGIES, M)
    green_list = []
    for layer_no in range(N_LAYER):
        incoming = solve_layer(levels, onsite[layer_no], broadening[layer_no], hamiltonian[layer_no], coupling[layer_no], coupling_mask[layer_no], prior_sigma[layer_no], incoming, NS_ITERS)
        green_list.append(incoming)
    kernel = convolution_matrix(kernel_weights, kernel_offsets, ENERGIES, ENERGIES, 0)
    outputs = [jnp.einsum("fe,epij->fpij", kernel, green_block, precision=exact_mode) for green_block in green_list]
    return jnp.stack(outputs)
```

```python
import functools

import jax
import jax.numpy as jnp
from jax import lax
from jax.experimental import pallas as pl
from jax.experimental.pallas import tpu as pltpu
from jax.sharding import PartitionSpec as P

MESH = pl.DeviceIdType.MESH
F32 = jnp.float32
BF16 = jnp.bfloat16
OWN = 4
SLOTS = 18
TAPS = 8


def split(value):
    high = value.astype(BF16)
    low = (value - high.astype(F32)).astype(BF16)
    return high, low


def dot(a, b):
    return jnp.dot(a, b, preferred_element_type=F32)


def product(first, second):
    fh, fl = first
    sh, sl = second
    n = sh.shape[0] // 2

    def against(part):
        rows = slice(part * n, (part + 1) * n)
        return dot(fh, sh[rows]) + (dot(fl, sh[rows]) + dot(fh, sl[rows]))

    real, imag = against(0), against(1)
    return real[:n] - imag[n:], real[n:] + imag[:n]


def kernel(
    layers,
    groups,
    onsite,
    broad,
    weights,
    offsets,
    ham,
    coup,
    mask,
    prior,
    out,
    prior_v,
    ham_v,
    coup_v,
    mask_v,
    slots,
    inc,
    acc,
    base,
    c_h,
    c_l,
    ch_h,
    ch_l,
    table,
    load_sem,
    prior_sem,
    xs_sem,
    xr_sem,
    near_sem,
    far_sem,
    skip_sem,
    fwd_sem,
    slot_sem,
    out_sem,
    token,
):
    n = onsite.shape[-1]
    x = lax.axis_index("layer")
    m = lax.axis_index("energy")
    odd = lax.rem(m, 2)
    sign = 1 - 2 * odd
    near = m + sign
    far = m - sign
    skip = m + 2 * sign
    behind = m - 2 * sign
    near_ok = jnp.logical_and(skip >= 0, skip < groups)
    far_ok = jnp.logical_and(far >= 0, far < groups)
    first_layer = x == 0
    has_next = x < layers - 1

    def place(t):
        return jnp.where(odd == 1, OWN - 1 - t, t)

    loads = [
        pltpu.make_async_copy(coup, coup_v, load_sem.at[0]),
        pltpu.make_async_copy(mask, mask_v, load_sem.at[1]),
        pltpu.make_async_copy(ham, ham_v, load_sem.at[2]),
    ]
    for load in loads:
        load.start()

    def prior_load(t):
        return pltpu.make_async_copy(prior.at[place(t)], prior_v.at[t], prior_sem.at[t])

    for t in range(OWN):
        prior_load(t).start()

    barrier = pltpu.get_barrier_semaphore()
    pl.semaphore_signal(barrier, inc=1, device_id=(x, near), device_id_type=MESH)

    @pl.when(far_ok)
    def _():
        pl.semaphore_signal(barrier, inc=1, device_id=(x, far), device_id_type=MESH)
        pl.semaphore_signal(barrier, inc=1, device_id=(x, behind), device_id_type=MESH)

    @pl.when(x > 0)
    def _():
        pl.semaphore_signal(barrier, inc=1, device_id=(x - 1, m), device_id_type=MESH)

    for i in range(SLOTS + 3):
        tap = F32(0.0)
        for j in range(TAPS):
            tap = tap + jnp.where(offsets[j] * sign == i - 10, weights[j], F32(0.0))
        table[i] = tap

    acc[...] = jnp.zeros_like(acc)

    @pl.when(jnp.logical_not(far_ok))
    def _():
        slots[0:7] = jnp.zeros((7, 2 * n, n), F32)

    @pl.when(jnp.logical_not(near_ok))
    def _():
        slots[15:18] = jnp.zeros((3, 2 * n, n), F32)

    loads[0].wait()
    loads[1].wait()
    kept = mask_v[...].astype(F32)
    c_real, c_imag = coup_v[:n] * kept, coup_v[n:] * kept
    for half, part in ((0, c_real), (1, c_imag)):
        c_h[half * n : (half + 1) * n], c_l[half * n : (half + 1) * n] = split(part)
    for half, part in ((0, c_real.T), (1, -c_imag.T)):
        ch_h[half * n : (half + 1) * n], ch_l[half * n : (half + 1) * n] = split(part)
    loads[2].wait()
    base[:n] = 0.5 * (ham_v[:n] + ham_v[:n].T)
    base[n:] = 0.5 * (ham_v[n:] - ham_v[n:].T)

    @pl.when(first_layer)
    def _():
        into = jnp.concatenate([0.5 * (coup_v[n:] * mask_v[...].astype(F32)), -0.5 * (coup_v[:n] * mask_v[...].astype(F32))])
        real, imag = product(split(into), (ch_h[...], ch_l[...]))
        base[:n] += real
        base[n:] += imag

    pl.semaphore_wait(
        barrier,
        1 + far_ok.astype(jnp.int32) + near_ok.astype(jnp.int32) + has_next.astype(jnp.int32),
    )

    rows_first = 3 * n // 2

    def to_next(t, part):
        rows = pl.ds(0, rows_first) if part == 0 else pl.ds(rows_first, 2 * n - rows_first)
        return pltpu.make_async_remote_copy(
            src_ref=slots.at[7 + t, rows],
            dst_ref=inc.at[t, rows],
            send_sem=xs_sem.at[t, part],
            recv_sem=xr_sem.at[t, part],
            device_id=(jnp.minimum(x + 1, layers - 1), m),
            device_id_type=MESH,
        )

    def send(source, target, send_sem, device):
        return pltpu.make_async_remote_copy(
            src_ref=slots.at[source],
            dst_ref=slots.at[target],
            send_sem=send_sem,
            recv_sem=slot_sem.at[target],
            device_id=(x, device),
            device_id_type=MESH,
        )

    def to_near(t):
        return send(7 + t, 14 - t, near_sem.at[t], near)

    def to_far(t):
        return send(7 + t, 6 - t, far_sem.at[t], far)

    def to_skip(t):
        return send(7 + t, t - 1, skip_sem.at[t], skip)

    def forward(t):
        return send(6 - t, 15 + t, fwd_sem.at[t], near)

    def arrived(slot):
        send(slot, slot, near_sem.at[0], near).wait_recv()

    def accumulate(sources):
        taps = [[table[u - v + 3] for v in range(OWN)] for u in sources]

        def body(c, carry):
            rows = pl.ds(pl.multiple_of(c * 16, 16), 16)
            blocks = [slots[u, rows, :] for u in sources]
            for v in range(OWN):
                total = acc[v, rows, :]
                for s in range(len(sources)):
                    total = total + taps[s][v] * blocks[s]
                acc[v, rows, :] = total
            return carry

        lax.fori_loop(0, 2 * n // 16, body, 0)

    def gather(t):
        @pl.when(far_ok)
        def _():
            arrived(6 - t)

            @pl.when(t < OWN - 1)
            def _():
                forward(t).start()

        arrived(14 - t)
        accumulate([7 + t, 14 - t, 6 - t])

        @pl.when(t > 0)
        def _():
            @pl.when(far_ok)
            def _():
                arrived(t - 1)

            @pl.when(near_ok)
            def _():
                arrived(14 + t)

            accumulate([t - 1, 14 + t])

    eye = lax.broadcasted_iota(jnp.int32, (n, n), 0) == lax.broadcasted_iota(jnp.int32, (n, n), 1)

    def step(t, carry):
        prior_load(t).wait()
        contact = slots.at[7 + t]

        @pl.when(first_layer)
        def _():
            contact[...] = base[...] + prior_v[t]

        @pl.when(jnp.logical_not(first_layer))
        def _():
            to_next(t, 0).wait_recv()
            to_next(t, 1).wait_recv()
            half_way = jnp.concatenate(product((c_h[...], c_l[...]), split(inc[t])))
            real, imag = product(split(half_way), (ch_h[...], ch_l[...]))
            contact[:n] = real + (base[:n] + prior_v[t, :n])
            contact[n:] = imag + (base[n:] + prior_v[t, n:])

        energy = (m * OWN + place(t)).astype(F32)
        level = -1.0 + 2.0 * (energy + 0.5) / (groups * OWN)
        real, imag = contact[:n], contact[n:]
        diag_real = (level - onsite[...]) - jnp.sum(jnp.where(eye, real, 0.0), axis=0, keepdims=True)
        diag_imag = broad[...] - jnp.sum(jnp.where(eye, imag, 0.0), axis=0, keepdims=True)
        modulus = diag_real * diag_real + diag_imag * diag_imag
        inv_real, inv_imag = diag_real / modulus, -diag_imag / modulus
        col_real = jnp.sum(jnp.where(eye, inv_real, 0.0), axis=1, keepdims=True)
        col_imag = jnp.sum(jnp.where(eye, inv_imag, 0.0), axis=1, keepdims=True)
        real, imag = jnp.where(eye, 0.0, real), jnp.where(eye, 0.0, imag)
        res_real = real * inv_real - imag * inv_imag
        res_imag = real * inv_imag + imag * inv_real
        one_real = jnp.where(eye, inv_real, col_real * res_real - col_imag * res_imag)
        one_imag = jnp.where(eye, inv_imag, col_real * res_imag + col_imag * res_real)
        residue = split(jnp.concatenate([res_real, res_imag]))
        square = jnp.concatenate(product(residue, residue))
        square = split(square)
        one = jnp.concatenate([one_real, one_imag])
        fourth = split(jnp.concatenate(product(square, square)))
        real, imag = product(split(one), square)
        two = one + jnp.concatenate([real, imag])
        real, imag = product(split(two), fourth)
        slots[7 + t] = two + jnp.concatenate([real, imag])

        @pl.when(far_ok)
        def _():
            to_far(t).start()

        @pl.when(jnp.logical_and(near_ok, t > 0))
        def _():
            to_skip(t).start()

        @pl.when(has_next)
        def _():
            @pl.when(jnp.logical_and(first_layer, t + odd > 0))
            def _():
                pl.semaphore_wait(token, 1)

            to_next(t, 0).start()
            to_next(t, 1).start()

        to_near(t).start()

        @pl.when(t > 0)
        def _():
            gather(t - 1)

        @pl.when(first_layer)
        def _():
            to_next(t, 0).wait_send()

            @pl.when(jnp.logical_or(odd == 0, t < OWN - 1))
            def _():
                pl.semaphore_signal(token, inc=1, device_id=(x, near), device_id_type=MESH)

        return carry

    lax.fori_loop(0, OWN, step, 0)
    gather(OWN - 1)

    stores = [
        pltpu.make_async_copy(acc.at[v], out.at[place(v)], out_sem.at[v]) for v in range(OWN)
    ]
    for store in stores:
        store.start()

    for t in range(OWN):
        to_near(t).wait_send()

        @pl.when(has_next)
        def _():
            @pl.when(jnp.logical_not(first_layer))
            def _():
                to_next(t, 0).wait_send()

            to_next(t, 1).wait_send()

        @pl.when(far_ok)
        def _():
            to_far(t).wait_send()
            if t < OWN - 1:
                forward(t).wait_send()

        if t > 0:

            @pl.when(near_ok)
            def _():
                to_skip(t).wait_send()

    for store in stores:
        store.wait()


def solution(mesh):
    layers, groups = mesh.shape["layer"], mesh.shape["energy"]

    def local(onsite, broad, ham, coup, mask, prior, weights, offsets):
        n = onsite.shape[-1]
        hbm = pl.BlockSpec(memory_space=pl.ANY)
        vmem = pl.BlockSpec(memory_space=pltpu.VMEM)
        smem = pl.BlockSpec(memory_space=pltpu.SMEM)
        block = (2 * n, n)
        result = pl.pallas_call(
            functools.partial(kernel, layers, groups),
            out_shape=jax.ShapeDtypeStruct((OWN, 2 * n, n), F32),
            in_specs=[vmem, vmem, smem, smem, hbm, hbm, hbm, hbm],
            out_specs=hbm,
            scratch_shapes=[
                pltpu.VMEM((OWN, *block), F32),
                pltpu.VMEM(block, F32),
                pltpu.VMEM(block, F32),
                pltpu.VMEM((n, n), jnp.int32),
                pltpu.VMEM((SLOTS, *block), F32),
                pltpu.VMEM((OWN, *block), F32),
                pltpu.VMEM((OWN, *block), F32),
                pltpu.VMEM(block, F32),
                pltpu.VMEM(block, BF16),
                pltpu.VMEM(block, BF16),
                pltpu.VMEM(block, BF16),
                pltpu.VMEM(block, BF16),
                pltpu.SMEM((SLOTS + 3,), F32),
                pltpu.SemaphoreType.DMA((3,)),
                pltpu.SemaphoreType.DMA((OWN,)),
                pltpu.SemaphoreType.DMA((OWN, 2)),
                pltpu.SemaphoreType.DMA((OWN, 2)),
                pltpu.SemaphoreType.DMA((OWN,)),
                pltpu.SemaphoreType.DMA((OWN,)),
                pltpu.SemaphoreType.DMA((OWN,)),
                pltpu.SemaphoreType.DMA((OWN,)),
                pltpu.SemaphoreType.DMA((SLOTS,)),
                pltpu.SemaphoreType.DMA((OWN,)),
                pltpu.SemaphoreType.REGULAR,
            ],
            compiler_params=pltpu.CompilerParams(
                collective_id=0, has_side_effects=True, vmem_limit_bytes=50 * 2**20
            ),
        )(
            onsite,
            broad,
            weights,
            offsets,
            ham.reshape(block),
            coup.reshape(block),
            mask.reshape(n, n),
            prior.reshape(OWN, *block),
        )
        return result.reshape(1, OWN, 2, n, n)

    return jax.shard_map(
        local,
        mesh=mesh,
        in_specs=(
            P("layer", None),
            P("layer", None),
            P("layer", None, None, None),
            P("layer", None, None, None),
            P("layer", None, None),
            P("layer", "energy", None, None, None),
            P(),
            P(),
        ),
        out_specs=P("layer", "energy", None, None, None),
        check_vma=False,
    )
```

```python
import functools

import jax
import jax.numpy as jnp
from jax import lax
from jax.experimental import pallas as pl
from jax.experimental.pallas import tpu as pltpu
from jax.sharding import PartitionSpec as P

MESH = pl.DeviceIdType.MESH
F32 = jnp.float32
BF16 = jnp.bfloat16
OWN = 4
SLOTS = 18
TAPS = 8


def split(value):
    high = value.astype(BF16)
    low = (value - high.astype(F32)).astype(BF16)
    return high, low


def dot(a, b):
    return jnp.dot(a, b, preferred_element_type=F32)


def halves(first, second, n):
    fh, fl = first
    sh, sl = second
    re, im = slice(0, n), slice(n, 2 * n)

    def three(rows, part):
        return dot(fh[rows], sh[part]) + (dot(fl[rows], sh[part]) + dot(fh[rows], sl[part]))

    yield three(re, re) - three(im, im)
    yield three(im, re) + three(re, im)


def kernel(
    layers,
    groups,
    onsite,
    broad,
    weights,
    offsets,
    ham,
    coup,
    mask,
    prior,
    out,
    onsite_v,
    broad_v,
    weights_s,
    offsets_s,
    prior_v,
    ham_v,
    coup_v,
    mask_v,
    slots,
    inc,
    acc,
    base,
    contact,
    one,
    two,
    pairs,
    table,
    load_sem,
    prior_sem,
    xs_sem,
    xr_sem,
    near_sem,
    far_sem,
    skip_sem,
    fwd_sem,
    slot_sem,
    out_sem,
    token,
):
    n = onsite.shape[-1]
    x = lax.axis_index("layer")
    m = lax.axis_index("energy")
    odd = lax.rem(m, 2)
    sign = 1 - 2 * odd
    near = m + sign
    far = m - sign
    skip = m + 2 * sign
    behind = m - 2 * sign
    near_ok = jnp.logical_and(skip >= 0, skip < groups)
    far_ok = jnp.logical_and(far >= 0, far < groups)
    first_layer = x == 0
    later_layer = x > 0
    has_next = x < layers - 1
    re, im = slice(0, n), slice(n, 2 * n)
    coupled, adjoint, along, residue, square, first_sum, fourth, second_sum = (
        (pairs.at[2 * i], pairs.at[2 * i + 1]) for i in range(8)
    )

    def keep(pair, rows, value):
        pair[0][rows], pair[1][rows] = split(value)

    def place(t):
        return jnp.where(odd == 1, OWN - 1 - t, t)

    def prior_load(t):
        return pltpu.make_async_copy(prior.at[place(t)], prior_v.at[t], prior_sem.at[t])

    loads = [
        pltpu.make_async_copy(source, target, load_sem.at[i])
        for i, (source, target) in enumerate(
            [
                (coup, coup_v),
                (mask, mask_v),
                (ham, ham_v),
                (onsite, onsite_v),
                (broad, broad_v),
                (weights, weights_s),
                (offsets, offsets_s),
            ]
        )
    ]
    for load in loads[:3]:
        load.start()
    prior_load(0).start()
    for load in loads[3:]:
        load.start()
    for t in range(1, OWN):
        prior_load(t).start()

    barrier = pltpu.get_barrier_semaphore()
    pl.semaphore_signal(barrier, inc=1, device_id=(x, near), device_id_type=MESH)

    @pl.when(far_ok)
    def _():
        pl.semaphore_signal(barrier, inc=1, device_id=(x, far), device_id_type=MESH)
        pl.semaphore_signal(barrier, inc=1, device_id=(x, behind), device_id_type=MESH)

    @pl.when(later_layer)
    def _():
        pl.semaphore_signal(barrier, inc=1, device_id=(x - 1, m), device_id_type=MESH)

    def prepare():
        acc[...] = jnp.zeros_like(acc)

        @pl.when(jnp.logical_not(far_ok))
        def _():
            slots[0:7] = jnp.zeros((7, 2 * n, n), F32)

        @pl.when(jnp.logical_not(near_ok))
        def _():
            slots[15:18] = jnp.zeros((3, 2 * n, n), F32)

        loads[5].wait()
        loads[6].wait()
        for i in range(SLOTS + 3):
            tap = F32(0.0)
            for j in range(TAPS):
                tap = tap + jnp.where(offsets_s[j] * sign == i - 10, weights_s[j], F32(0.0))
            table[i] = tap

    loads[0].wait()
    loads[1].wait()
    kept = mask_v[...].astype(F32)
    coup_v[re] = coup_v[re] * kept
    coup_v[im] = coup_v[im] * kept
    keep(coupled, re, coup_v[re])
    keep(coupled, im, coup_v[im])
    keep(adjoint, re, coup_v[re].T)
    keep(adjoint, im, -coup_v[im].T)
    loads[2].wait()
    base[re] = 0.5 * (ham_v[re] + ham_v[re].T)
    base[im] = 0.5 * (ham_v[im] - ham_v[im].T)
    loads[3].wait()
    loads[4].wait()

    @pl.when(first_layer)
    def _():
        keep(along, re, 0.5 * coup_v[im])
        keep(along, im, -0.5 * coup_v[re])
        for rows, part in zip((re, im), halves(along, adjoint, n)):
            base[rows] += part

    @pl.when(later_layer)
    def _():
        prepare()

    pl.semaphore_wait(
        barrier,
        1 + far_ok.astype(jnp.int32) + near_ok.astype(jnp.int32) + has_next.astype(jnp.int32),
    )

    quarter = n // 2

    def to_next(t, part):
        rows = pl.ds(part * quarter, quarter)
        return pltpu.make_async_remote_copy(
            src_ref=slots.at[7 + t, rows],
            dst_ref=inc.at[t, rows],
            send_sem=xs_sem.at[t, part],
            recv_sem=xr_sem.at[t, part],
            device_id=(jnp.minimum(x + 1, layers - 1), m),
            device_id_type=MESH,
        )

    def send(source, target, send_sem, device):
        return pltpu.make_async_remote_copy(
            src_ref=slots.at[source],
            dst_ref=slots.at[target],
            send_sem=send_sem,
            recv_sem=slot_sem.at[target],
            device_id=(x, device),
            device_id_type=MESH,
        )

    def to_near(t):
        return send(7 + t, 14 - t, near_sem.at[t], near)

    def to_far(t):
        return send(7 + t, 6 - t, far_sem.at[t], far)

    def to_skip(t):
        return send(7 + t, t - 1, skip_sem.at[t], skip)

    def forward(t):
        return send(6 - t, 15 + t, fwd_sem.at[t], near)

    def arrived(slot):
        send(slot, slot, near_sem.at[0], near).wait_recv()

    def accumulate(sources):
        taps = [[table[u - v + 3] for v in range(OWN)] for u in sources]

        def body(c, carry):
            rows = pl.ds(pl.multiple_of(c * 16, 16), 16)
            blocks = [slots[u, rows, :] for u in sources]
            for v in range(OWN):
                total = acc[v, rows, :]
                for s in range(len(sources)):
                    total = total + taps[s][v] * blocks[s]
                acc[v, rows, :] = total
            return carry

        lax.fori_loop(0, 2 * n // 16, body, 0)

    def gather(t):
        @pl.when(far_ok)
        def _():
            arrived(6 - t)

            @pl.when(t < OWN - 1)
            def _():
                forward(t).start()

        arrived(14 - t)
        accumulate([7 + t, 14 - t, 6 - t])

        @pl.when(t > 0)
        def _():
            @pl.when(far_ok)
            def _():
                arrived(t - 1)

            @pl.when(near_ok)
            def _():
                arrived(14 + t)

            accumulate([t - 1, 14 + t])

    eye = lax.broadcasted_iota(jnp.int32, (n, n), 0) == lax.broadcasted_iota(jnp.int32, (n, n), 1)

    def reciprocal(diag_real, diag_imag):
        modulus = diag_real * diag_real + diag_imag * diag_imag
        columns = diag_real / modulus, -diag_imag / modulus
        return [
            (column, jnp.sum(jnp.where(eye, column, 0.0), axis=0, keepdims=True))
            for column in columns
        ]

    def start_sweeps(q, size, real, imag, inverse):
        rows = slice(q * size, (q + 1) * size)
        (col_real, row_real), (col_imag, row_imag) = inverse
        on = eye[rows]
        real, imag = jnp.where(on, 0.0, real), jnp.where(on, 0.0, imag)
        res_real = real * row_real - imag * row_imag
        res_imag = real * row_imag + imag * row_real
        keep(residue, rows, res_real)
        keep(residue, slice(n + q * size, n + (q + 1) * size), res_imag)
        cr, ci = col_real[rows], col_imag[rows]
        one[q * size : (q + 1) * size] = jnp.where(on, row_real, cr * res_real - ci * res_imag)
        one[n + q * size : n + (q + 1) * size] = jnp.where(on, row_imag, cr * res_imag + ci * res_real)

    def step(t, carry):
        prior_load(t).wait()
        energy = (m * OWN + place(t)).astype(F32)
        level = -1.0 + 2.0 * (energy + 0.5) / (groups * OWN)
        contact[...] = base[...] + prior_v[t]
        diag_real = jnp.sum(jnp.where(eye, (level - onsite_v[...]) - contact[re], 0.0), axis=1, keepdims=True)
        diag_imag = jnp.sum(jnp.where(eye, broad_v[...] - contact[im], 0.0), axis=1, keepdims=True)

        @pl.when(first_layer)
        def _():
            start_sweeps(0, n, contact[re], contact[im], reciprocal(diag_real, diag_imag))

        @pl.when(later_layer)
        def _():
            to_next(t, 0).wait_recv()
            to_next(t, 1).wait_recv()
            (ch, cl), (in_h, in_l) = coupled, fourth
            keep(fourth, re, inc[t, re])
            left = dot(ch[...], in_h[re]) + (dot(cl[...], in_h[re]) + dot(ch[...], in_l[re]))
            to_next(t, 2).wait_recv()
            to_next(t, 3).wait_recv()
            keep(fourth, im, inc[t, im])
            right = dot(ch[...], in_h[im]) + (dot(cl[...], in_h[im]) + dot(ch[...], in_l[im]))
            way_real, way_imag = left[re] - right[im], left[im] + right[re]
            keep(along, re, way_real)
            keep(along, im, way_imag)
            c_real, c_imag = coup_v[re], coup_v[im]
            inverse = reciprocal(
                diag_real - jnp.sum(way_real * c_real + way_imag * c_imag, axis=1, keepdims=True),
                diag_imag - jnp.sum(way_imag * c_real - way_real * c_imag, axis=1, keepdims=True),
            )
            size = n // 2
            (ah, al), (dh, dl) = along, adjoint
            for q in range(2):
                top, low = slice(q * size, (q + 1) * size), slice(n + q * size, n + (q + 1) * size)

                def three(rows, part):
                    return dot(ah[rows], dh[part]) + (dot(al[rows], dh[part]) + dot(ah[rows], dl[part]))

                real = three(top, re) - three(low, im) + contact[top]
                imag = three(low, re) + three(top, im) + contact[low]
                start_sweeps(q, size, real, imag, inverse)

        for rows, part in zip((re, im), halves(residue, residue, n)):
            keep(square, rows, part)
        for rows in (re, im):
            keep(first_sum, rows, one[rows])
        for rows, part in zip((re, im), halves(first_sum, square, n)):
            two[rows] = one[rows] + part
            keep(second_sum, rows, two[rows])
        for rows, part in zip((re, im), halves(square, square, n)):
            keep(fourth, rows, part)
        at_once = jnp.logical_and(has_next, jnp.logical_or(later_layer, t + odd == 0))
        for parts, rows, part in zip(((0, 1), (2, 3)), (re, im), halves(second_sum, fourth, n)):
            slots[7 + t, rows] = two[rows] + part

            @pl.when(at_once)
            def _():
                for p in parts:
                    to_next(t, p).start()

        @pl.when(far_ok)
        def _():
            to_far(t).start()

        @pl.when(jnp.logical_and(near_ok, t > 0))
        def _():
            to_skip(t).start()

        to_near(t).start()

        @pl.when(jnp.logical_and(first_layer, t + odd > 0))
        def _():
            pl.semaphore_wait(token, 1)
            for p in range(4):
                to_next(t, p).start()

        @pl.when(jnp.logical_and(first_layer, t == 0))
        def _():
            prepare()

        @pl.when(t > 0)
        def _():
            gather(t - 1)

        @pl.when(first_layer)
        def _():
            for p in range(3):
                to_next(t, p).wait_send()

            @pl.when(jnp.logical_or(odd == 0, t < OWN - 1))
            def _():
                pl.semaphore_signal(token, inc=1, device_id=(x, near), device_id_type=MESH)

        return carry

    lax.fori_loop(0, OWN, step, 0)
    gather(OWN - 1)

    stores = [
        pltpu.make_async_copy(acc.at[v], out.at[place(v)], out_sem.at[v]) for v in range(OWN)
    ]
    for store in stores:
        store.start()

    for t in range(OWN):
        to_near(t).wait_send()

        @pl.when(has_next)
        def _():
            @pl.when(later_layer)
            def _():
                for p in range(3):
                    to_next(t, p).wait_send()

            to_next(t, 3).wait_send()

        @pl.when(far_ok)
        def _():
            to_far(t).wait_send()
            if t < OWN - 1:
                forward(t).wait_send()

        if t > 0:

            @pl.when(near_ok)
            def _():
                to_skip(t).wait_send()

    for store in stores:
        store.wait()


def solution(mesh):
    layers, groups = mesh.shape["layer"], mesh.shape["energy"]

    def local(onsite, broad, ham, coup, mask, prior, weights, offsets):
        n = onsite.shape[-1]
        hbm = pl.BlockSpec(memory_space=pltpu.HBM)
        block = (2 * n, n)
        result = pl.pallas_call(
            functools.partial(kernel, layers, groups),
            out_shape=jax.ShapeDtypeStruct((OWN, 2 * n, n), F32),
            in_specs=[hbm] * 8,
            out_specs=hbm,
            scratch_shapes=[
                pltpu.VMEM((1, n), F32),
                pltpu.VMEM((1, n), F32),
                pltpu.SMEM((TAPS,), F32),
                pltpu.SMEM((TAPS,), jnp.int32),
                pltpu.VMEM((OWN, *block), F32),
                pltpu.VMEM(block, F32),
                pltpu.VMEM(block, F32),
                pltpu.VMEM((n, n), jnp.int32),
                pltpu.VMEM((SLOTS, *block), F32),
                pltpu.VMEM((OWN, *block), F32),
                pltpu.VMEM((OWN, *block), F32),
                pltpu.VMEM(block, F32),
                pltpu.VMEM(block, F32),
                pltpu.VMEM(block, F32),
                pltpu.VMEM(block, F32),
                pltpu.VMEM((16, *block), BF16),
                pltpu.SMEM((SLOTS + 3,), F32),
                pltpu.SemaphoreType.DMA((7,)),
                pltpu.SemaphoreType.DMA((OWN,)),
                pltpu.SemaphoreType.DMA((OWN, 4)),
                pltpu.SemaphoreType.DMA((OWN, 4)),
                pltpu.SemaphoreType.DMA((OWN,)),
                pltpu.SemaphoreType.DMA((OWN,)),
                pltpu.SemaphoreType.DMA((OWN,)),
                pltpu.SemaphoreType.DMA((OWN,)),
                pltpu.SemaphoreType.DMA((SLOTS,)),
                pltpu.SemaphoreType.DMA((OWN,)),
                pltpu.SemaphoreType.REGULAR,
            ],
            compiler_params=pltpu.CompilerParams(
                collective_id=0, has_side_effects=True, vmem_limit_bytes=62 * 2**20
            ),
        )(
            onsite,
            broad,
            weights,
            offsets,
            ham.reshape(block),
            coup.reshape(block),
            mask.reshape(n, n),
            prior.reshape(OWN, *block),
        )
        return result.reshape(1, OWN, 2, n, n)

    return jax.shard_map(
        local,
        mesh=mesh,
        in_specs=(
            P("layer", None),
            P("layer", None),
            P("layer", None, None, None),
            P("layer", None, None, None),
            P("layer", None, None),
            P("layer", "energy", None, None, None),
            P(),
            P(),
        ),
        out_specs=P("layer", "energy", None, None, None),
        check_vma=False,
    )
```

```python
import functools

import jax
import jax.numpy as jnp
from jax import lax
from jax.experimental import pallas as pl
from jax.experimental.pallas import tpu as pltpu
from jax.sharding import PartitionSpec as P

MESH = pl.DeviceIdType.MESH
F32 = jnp.float32
BF16 = jnp.bfloat16
OWN = 4
SLOTS = 18
TAPS = 8


def split(value):
    high = value.astype(BF16)
    low = (value - high.astype(F32)).astype(BF16)
    return high, low


def dot(a, b):
    return jnp.dot(a, b, preferred_element_type=F32)


def halves(first, second, n):
    fh, fl = first
    sh, sl = second
    re, im = slice(0, n), slice(n, 2 * n)

    def three(rows, part):
        return dot(fh[rows], sh[part]) + (dot(fl[rows], sh[part]) + dot(fh[rows], sl[part]))

    yield three(re, re) - three(im, im)
    yield three(im, re) + three(re, im)


def row_chunks(first, second, n, count=2):
    fh, fl = first
    sh, sl = second
    re, im = slice(0, n), slice(n, 2 * n)

    def three(rows, part):
        return dot(fh[rows], sh[part]) + (dot(fl[rows], sh[part]) + dot(fh[rows], sl[part]))

    size = n // count
    for q in range(count):
        top, low = slice(q * size, (q + 1) * size), slice(n + q * size, n + (q + 1) * size)
        yield top, low, three(top, re) - three(low, im), three(low, re) + three(top, im)


def kernel(
    layers,
    groups,
    onsite,
    broad,
    weights,
    offsets,
    ham,
    coup,
    mask,
    prior,
    out,
    onsite_v,
    broad_v,
    weights_s,
    offsets_s,
    prior_v,
    ham_v,
    coup_v,
    mask_v,
    slots,
    inc,
    acc,
    base,
    contact,
    one,
    two,
    pairs,
    table,
    load_sem,
    prior_sem,
    xs_sem,
    xr_sem,
    near_sem,
    far_sem,
    skip_sem,
    fwd_sem,
    slot_sem,
    out_sem,
    token,
):
    n = onsite.shape[-1]
    x = lax.axis_index("layer")
    m = lax.axis_index("energy")
    odd = lax.rem(m, 2)
    sign = 1 - 2 * odd
    near = m + sign
    far = m - sign
    skip = m + 2 * sign
    behind = m - 2 * sign
    near_ok = jnp.logical_and(skip >= 0, skip < groups)
    far_ok = jnp.logical_and(far >= 0, far < groups)
    first_layer = x == 0
    later_layer = x > 0
    has_next = x < layers - 1
    re, im = slice(0, n), slice(n, 2 * n)
    coupled, adjoint, along, residue, square, first_sum, fourth, second_sum = (
        (pairs.at[2 * i], pairs.at[2 * i + 1]) for i in range(8)
    )

    def keep(pair, rows, value):
        pair[0][rows], pair[1][rows] = split(value)

    def place(t):
        return jnp.where(odd == 1, OWN - 1 - t, t)

    def prior_load(t):
        return pltpu.make_async_copy(prior.at[place(t)], prior_v.at[t], prior_sem.at[t])

    loads = [
        pltpu.make_async_copy(source, target, load_sem.at[i])
        for i, (source, target) in enumerate(
            [
                (coup, coup_v),
                (mask, mask_v),
                (ham, ham_v),
                (onsite, onsite_v),
                (broad, broad_v),
                (weights, weights_s),
                (offsets, offsets_s),
            ]
        )
    ]
    for load in loads[:3]:
        load.start()
    prior_load(0).start()
    for load in loads[3:]:
        load.start()
    for t in range(1, OWN):
        prior_load(t).start()

    barrier = pltpu.get_barrier_semaphore()
    pl.semaphore_signal(barrier, inc=1, device_id=(x, near), device_id_type=MESH)

    @pl.when(far_ok)
    def _():
        pl.semaphore_signal(barrier, inc=1, device_id=(x, far), device_id_type=MESH)
        pl.semaphore_signal(barrier, inc=1, device_id=(x, behind), device_id_type=MESH)

    @pl.when(later_layer)
    def _():
        pl.semaphore_signal(barrier, inc=1, device_id=(x - 1, m), device_id_type=MESH)

    def prepare():
        acc[...] = jnp.zeros_like(acc)

        @pl.when(jnp.logical_not(far_ok))
        def _():
            slots[0:7] = jnp.zeros((7, 2 * n, n), F32)

        @pl.when(jnp.logical_not(near_ok))
        def _():
            slots[15:18] = jnp.zeros((3, 2 * n, n), F32)

        loads[5].wait()
        loads[6].wait()
        for i in range(SLOTS + 3):
            tap = F32(0.0)
            for j in range(TAPS):
                tap = tap + jnp.where(offsets_s[j] * sign == i - 10, weights_s[j], F32(0.0))
            table[i] = tap

    loads[0].wait()
    loads[1].wait()
    kept = mask_v[...].astype(F32)
    coup_v[re] = coup_v[re] * kept
    coup_v[im] = coup_v[im] * kept
    keep(coupled, re, coup_v[re])
    keep(coupled, im, coup_v[im])
    keep(adjoint, re, coup_v[re].T)
    keep(adjoint, im, -coup_v[im].T)
    loads[2].wait()
    base[re] = 0.5 * (ham_v[re] + ham_v[re].T)
    base[im] = 0.5 * (ham_v[im] - ham_v[im].T)
    loads[3].wait()
    loads[4].wait()

    @pl.when(first_layer)
    def _():
        keep(along, re, 0.5 * coup_v[im])
        keep(along, im, -0.5 * coup_v[re])
        for rows, part in zip((re, im), halves(along, adjoint, n)):
            base[rows] += part

    @pl.when(later_layer)
    def _():
        prepare()

    pl.semaphore_wait(
        barrier,
        1 + far_ok.astype(jnp.int32) + near_ok.astype(jnp.int32) + has_next.astype(jnp.int32),
    )

    quarter = n // 2

    def to_next(t, part):
        rows = pl.ds(part * quarter, quarter)
        return pltpu.make_async_remote_copy(
            src_ref=slots.at[7 + t, rows],
            dst_ref=inc.at[t, rows],
            send_sem=xs_sem.at[t, part],
            recv_sem=xr_sem.at[t, part],
            device_id=(jnp.minimum(x + 1, layers - 1), m),
            device_id_type=MESH,
        )

    def send(source, target, send_sem, device):
        return pltpu.make_async_remote_copy(
            src_ref=slots.at[source],
            dst_ref=slots.at[target],
            send_sem=send_sem,
            recv_sem=slot_sem.at[target],
            device_id=(x, device),
            device_id_type=MESH,
        )

    def to_near(t):
        return send(7 + t, 14 - t, near_sem.at[t], near)

    def to_far(t):
        return send(7 + t, 6 - t, far_sem.at[t], far)

    def to_skip(t):
        return send(7 + t, t - 1, skip_sem.at[t], skip)

    def forward(t):
        return send(6 - t, 15 + t, fwd_sem.at[t], near)

    def arrived(slot):
        send(slot, slot, near_sem.at[0], near).wait_recv()

    def accumulate(sources):
        taps = [[table[u - v + 3] for v in range(OWN)] for u in sources]

        def body(c, carry):
            rows = pl.ds(pl.multiple_of(c * 16, 16), 16)
            blocks = [slots[u, rows, :] for u in sources]
            for v in range(OWN):
                total = acc[v, rows, :]
                for s in range(len(sources)):
                    total = total + taps[s][v] * blocks[s]
                acc[v, rows, :] = total
            return carry

        lax.fori_loop(0, 2 * n // 16, body, 0)

    def gather(t):
        @pl.when(far_ok)
        def _():
            arrived(6 - t)

            @pl.when(t < OWN - 1)
            def _():
                forward(t).start()

        arrived(14 - t)
        accumulate([7 + t, 14 - t, 6 - t])

        @pl.when(t > 0)
        def _():
            @pl.when(far_ok)
            def _():
                arrived(t - 1)

            @pl.when(near_ok)
            def _():
                arrived(14 + t)

            accumulate([t - 1, 14 + t])

    eye = lax.broadcasted_iota(jnp.int32, (n, n), 0) == lax.broadcasted_iota(jnp.int32, (n, n), 1)

    def reciprocal(diag_real, diag_imag):
        modulus = diag_real * diag_real + diag_imag * diag_imag
        columns = diag_real / modulus, -diag_imag / modulus
        return [
            (column, jnp.sum(jnp.where(eye, column, 0.0), axis=0, keepdims=True))
            for column in columns
        ]

    def start_sweeps(q, size, real, imag, inverse):
        rows = slice(q * size, (q + 1) * size)
        (col_real, row_real), (col_imag, row_imag) = inverse
        on = eye[rows]
        real, imag = jnp.where(on, 0.0, real), jnp.where(on, 0.0, imag)
        res_real = real * row_real - imag * row_imag
        res_imag = real * row_imag + imag * row_real
        keep(residue, rows, res_real)
        keep(residue, slice(n + q * size, n + (q + 1) * size), res_imag)
        cr, ci = col_real[rows], col_imag[rows]
        one[q * size : (q + 1) * size] = jnp.where(on, row_real, cr * res_real - ci * res_imag)
        one[n + q * size : n + (q + 1) * size] = jnp.where(on, row_imag, cr * res_imag + ci * res_real)

    def step(t, carry):
        prior_load(t).wait()
        energy = (m * OWN + place(t)).astype(F32)
        level = -1.0 + 2.0 * (energy + 0.5) / (groups * OWN)
        contact[...] = base[...] + prior_v[t]
        diag_real = jnp.sum(jnp.where(eye, (level - onsite_v[...]) - contact[re], 0.0), axis=1, keepdims=True)
        diag_imag = jnp.sum(jnp.where(eye, broad_v[...] - contact[im], 0.0), axis=1, keepdims=True)

        @pl.when(first_layer)
        def _():
            start_sweeps(0, n, contact[re], contact[im], reciprocal(diag_real, diag_imag))

        @pl.when(later_layer)
        def _():
            to_next(t, 0).wait_recv()
            to_next(t, 1).wait_recv()
            (ch, cl), (in_h, in_l) = coupled, fourth
            keep(fourth, re, inc[t, re])
            left = dot(ch[...], in_h[re]) + (dot(cl[...], in_h[re]) + dot(ch[...], in_l[re]))
            to_next(t, 2).wait_recv()
            to_next(t, 3).wait_recv()
            keep(fourth, im, inc[t, im])
            size = n // 2
            diagonals = []
            for q in range(2):
                top, low = slice(q * size, (q + 1) * size), slice(n + q * size, n + (q + 1) * size)

                def right(rows):
                    return dot(ch[rows], in_h[im]) + (dot(cl[rows], in_h[im]) + dot(ch[rows], in_l[im]))

                way_real, way_imag = left[top] - right(low), left[low] + right(top)
                keep(along, top, way_real)
                keep(along, low, way_imag)
                diagonals.append(
                    (
                        jnp.sum(way_real * coup_v[top] + way_imag * coup_v[low], axis=1, keepdims=True),
                        jnp.sum(way_imag * coup_v[top] - way_real * coup_v[low], axis=1, keepdims=True),
                    )
                )
            on_real, on_imag = (jnp.concatenate([d[i] for d in diagonals]) for i in range(2))
            inverse = reciprocal(diag_real - on_real, diag_imag - on_imag)
            for q, (top, low, real, imag) in enumerate(row_chunks(along, adjoint, n)):
                start_sweeps(q, size, real + contact[top], imag + contact[low], inverse)

        for top, low, real, imag in row_chunks(residue, residue, n):
            keep(square, top, real)
            keep(square, low, imag)
        for top, low, real, imag in row_chunks(square, square, n):
            keep(fourth, top, real)
            keep(fourth, low, imag)
        for rows in (re, im):
            keep(first_sum, rows, one[rows])
        for top, low, real, imag in row_chunks(first_sum, square, n):
            two[top] = one[top] + real
            two[low] = one[low] + imag
            keep(second_sum, top, two[top])
            keep(second_sum, low, two[low])
        at_once = jnp.logical_and(has_next, jnp.logical_or(later_layer, t + odd == 0))
        for q, (top, low, real, imag) in enumerate(row_chunks(second_sum, fourth, n)):
            slots[7 + t, top] = two[top] + real
            slots[7 + t, low] = two[low] + imag

            @pl.when(at_once)
            def _():
                to_next(t, q).start()
                to_next(t, 2 + q).start()

        @pl.when(far_ok)
        def _():
            to_far(t).start()

        @pl.when(jnp.logical_and(near_ok, t > 0))
        def _():
            to_skip(t).start()

        to_near(t).start()

        @pl.when(jnp.logical_and(first_layer, t + odd > 0))
        def _():
            pl.semaphore_wait(token, 1)
            for p in range(4):
                to_next(t, p).start()

        @pl.when(jnp.logical_and(first_layer, t == 0))
        def _():
            prepare()

        @pl.when(t > 0)
        def _():
            gather(t - 1)

        @pl.when(first_layer)
        def _():
            for p in range(3):
                to_next(t, p).wait_send()

            @pl.when(jnp.logical_or(odd == 0, t < OWN - 1))
            def _():
                pl.semaphore_signal(token, inc=1, device_id=(x, near), device_id_type=MESH)

        return carry

    lax.fori_loop(0, OWN, step, 0)
    gather(OWN - 1)

    stores = [
        pltpu.make_async_copy(acc.at[v], out.at[place(v)], out_sem.at[v]) for v in range(OWN)
    ]
    for store in stores:
        store.start()

    for t in range(OWN):
        to_near(t).wait_send()

        @pl.when(has_next)
        def _():
            @pl.when(later_layer)
            def _():
                for p in range(3):
                    to_next(t, p).wait_send()

            to_next(t, 3).wait_send()

        @pl.when(far_ok)
        def _():
            to_far(t).wait_send()
            if t < OWN - 1:
                forward(t).wait_send()

        if t > 0:

            @pl.when(near_ok)
            def _():
                to_skip(t).wait_send()

    for store in stores:
        store.wait()


def solution(mesh):
    layers, groups = mesh.shape["layer"], mesh.shape["energy"]

    def local(onsite, broad, ham, coup, mask, prior, weights, offsets):
        n = onsite.shape[-1]
        hbm = pl.BlockSpec(memory_space=pltpu.HBM)
        block = (2 * n, n)
        result = pl.pallas_call(
            functools.partial(kernel, layers, groups),
            out_shape=jax.ShapeDtypeStruct((OWN, 2 * n, n), F32),
            in_specs=[hbm] * 8,
            out_specs=hbm,
            scratch_shapes=[
                pltpu.VMEM((1, n), F32),
                pltpu.VMEM((1, n), F32),
                pltpu.SMEM((TAPS,), F32),
                pltpu.SMEM((TAPS,), jnp.int32),
                pltpu.VMEM((OWN, *block), F32),
                pltpu.VMEM(block, F32),
                pltpu.VMEM(block, F32),
                pltpu.VMEM((n, n), jnp.int32),
                pltpu.VMEM((SLOTS, *block), F32),
                pltpu.VMEM((OWN, *block), F32),
                pltpu.VMEM((OWN, *block), F32),
                pltpu.VMEM(block, F32),
                pltpu.VMEM(block, F32),
                pltpu.VMEM(block, F32),
                pltpu.VMEM(block, F32),
                pltpu.VMEM((16, *block), BF16),
                pltpu.SMEM((SLOTS + 3,), F32),
                pltpu.SemaphoreType.DMA((7,)),
                pltpu.SemaphoreType.DMA((OWN,)),
                pltpu.SemaphoreType.DMA((OWN, 4)),
                pltpu.SemaphoreType.DMA((OWN, 4)),
                pltpu.SemaphoreType.DMA((OWN,)),
                pltpu.SemaphoreType.DMA((OWN,)),
                pltpu.SemaphoreType.DMA((OWN,)),
                pltpu.SemaphoreType.DMA((OWN,)),
                pltpu.SemaphoreType.DMA((SLOTS,)),
                pltpu.SemaphoreType.DMA((OWN,)),
                pltpu.SemaphoreType.REGULAR,
            ],
            compiler_params=pltpu.CompilerParams(
                collective_id=0, has_side_effects=True, vmem_limit_bytes=50 * 2**20
            ),
        )(
            *(
                pltpu.with_memory_space_constraint(v, pltpu.HBM)
                for v in (
                    onsite,
                    broad,
                    weights,
                    offsets,
                    ham.reshape(block),
                    coup.reshape(block),
                    mask.reshape(n, n),
                    prior.reshape(OWN, *block),
                )
            ),
        )
        return result.reshape(1, OWN, 2, n, n)

    return jax.shard_map(
        local,
        mesh=mesh,
        in_specs=(
            P("layer", None),
            P("layer", None),
            P("layer", None, None, None),
            P("layer", None, None, None),
            P("layer", None, None),
            P("layer", "energy", None, None, None),
            P(),
            P(),
        ),
        out_specs=P("layer", "energy", None, None, None),
        check_vma=False,
    )
```

```python
import functools

import jax
import jax.numpy as jnp
from jax import lax
from jax.experimental import pallas as pl
from jax.experimental.pallas import tpu as pltpu
from jax.sharding import PartitionSpec as P

MESH = pl.DeviceIdType.MESH
F32 = jnp.float32
BF16 = jnp.bfloat16
OWN = 4
SLOTS = 18
TAPS = 8


def split(value):
    high = value.astype(BF16)
    low = (value - high.astype(F32)).astype(BF16)
    return high, low


def dot(a, b):
    return jnp.dot(a, b, preferred_element_type=F32)


def halves(first, second, n):
    fh, fl = first
    sh, sl = second
    re, im = slice(0, n), slice(n, 2 * n)

    def three(rows, part):
        return dot(fh[rows], sh[part]) + (dot(fl[rows], sh[part]) + dot(fh[rows], sl[part]))

    yield three(re, re) - three(im, im)
    yield three(im, re) + three(re, im)


def row_chunks(first, second, n, count=2):
    fh, fl = first
    sh, sl = second
    re, im = slice(0, n), slice(n, 2 * n)

    def three(rows, part):
        return dot(fh[rows], sh[part]) + (dot(fl[rows], sh[part]) + dot(fh[rows], sl[part]))

    size = n // count
    for q in range(count):
        top, low = slice(q * size, (q + 1) * size), slice(n + q * size, n + (q + 1) * size)
        yield top, low, three(top, re) - three(low, im), three(low, re) + three(top, im)


def kernel(
    layers,
    groups,
    onsite,
    broad,
    weights,
    offsets,
    ham,
    coup,
    mask,
    prior,
    out,
    onsite_v,
    broad_v,
    weights_s,
    offsets_s,
    prior_v,
    ham_v,
    coup_v,
    mask_v,
    slots,
    inc,
    acc,
    base,
    contact,
    one,
    two,
    again_base,
    again_coup,
    again_prior,
    pairs,
    table,
    load_sem,
    prior_sem,
    xs_sem,
    xr_sem,
    near_sem,
    far_sem,
    skip_sem,
    fwd_sem,
    slot_sem,
    last_send,
    last_recv,
    twice_sem,
    const_send,
    const_recv,
    share_send,
    share_recv,
    again_send,
    again_recv,
    token,
):
    n = onsite.shape[-1]
    x = lax.axis_index("layer")
    m = lax.axis_index("energy")
    odd = lax.rem(m, 2)
    sign = 1 - 2 * odd
    near = m + sign
    far = m - sign
    skip = m + 2 * sign
    behind = m - 2 * sign
    near_ok = jnp.logical_and(skip >= 0, skip < groups)
    far_ok = jnp.logical_and(far >= 0, far < groups)
    first_layer = x == 0
    later_layer = x > 0
    has_next = x < layers - 2
    sends_twice = x == layers - 3
    constants_on = x == layers - 2
    last_layer = x == layers - 1
    re, im = slice(0, n), slice(n, 2 * n)
    coupled, adjoint, along, residue, square, first_sum, fourth, second_sum = (
        (pairs.at[2 * i], pairs.at[2 * i + 1]) for i in range(8)
    )
    again_coupled, again_adjoint = ((pairs.at[2 * i], pairs.at[2 * i + 1]) for i in (8, 9))

    def keep(pair, rows, value):
        pair[0][rows], pair[1][rows] = split(value)

    def place(t):
        return jnp.where(odd == 1, OWN - 1 - t, t)

    def prior_load(t):
        return pltpu.make_async_copy(prior.at[place(t)], prior_v.at[t], prior_sem.at[t])

    loads = [
        pltpu.make_async_copy(source, target, load_sem.at[i])
        for i, (source, target) in enumerate(
            [
                (coup, coup_v),
                (mask, mask_v),
                (ham, ham_v),
                (onsite, onsite_v),
                (broad, broad_v),
                (weights, weights_s),
                (offsets, offsets_s),
            ]
        )
    ]
    for load in loads[:3]:
        load.start()
    prior_load(0).start()
    for load in loads[3:]:
        load.start()
    for t in range(1, OWN):
        prior_load(t).start()

    barrier = pltpu.get_barrier_semaphore()
    pl.semaphore_signal(barrier, inc=1, device_id=(x, near), device_id_type=MESH)

    @pl.when(far_ok)
    def _():
        pl.semaphore_signal(barrier, inc=1, device_id=(x, far), device_id_type=MESH)
        pl.semaphore_signal(barrier, inc=1, device_id=(x, behind), device_id_type=MESH)

    @pl.when(later_layer)
    def _():
        pl.semaphore_signal(barrier, inc=1, device_id=(x - 1, m), device_id_type=MESH)

    @pl.when(last_layer)
    def _():
        pl.semaphore_signal(barrier, inc=1, device_id=(layers - 3, m), device_id_type=MESH)

    def prepare():
        acc[...] = jnp.zeros_like(acc)

        @pl.when(jnp.logical_not(far_ok))
        def _():
            slots[0:7] = jnp.zeros((7, 2 * n, n), F32)

        @pl.when(jnp.logical_not(near_ok))
        def _():
            slots[15:18] = jnp.zeros((3, 2 * n, n), F32)

        loads[5].wait()
        loads[6].wait()
        for i in range(SLOTS + 3):
            tap = F32(0.0)
            for j in range(TAPS):
                tap = tap + jnp.where(offsets_s[j] * sign == i - 10, weights_s[j], F32(0.0))
            table[i] = tap

    loads[0].wait()
    loads[1].wait()
    kept = mask_v[...].astype(F32)
    coup_v[re] = coup_v[re] * kept
    coup_v[im] = coup_v[im] * kept

    def factors(source, left, right):
        keep(left, re, source[re])
        keep(left, im, source[im])
        keep(right, re, source[re].T)
        keep(right, im, -source[im].T)

    factors(coup_v, coupled, adjoint)
    for load in loads[2:5]:
        load.wait()
    eye = lax.broadcasted_iota(jnp.int32, (n, n), 0) == lax.broadcasted_iota(jnp.int32, (n, n), 1)
    base[re] = 0.5 * (ham_v[re] + ham_v[re].T) + jnp.where(eye, onsite_v[...], 0.0)
    base[im] = 0.5 * (ham_v[im] - ham_v[im].T) - jnp.where(eye, broad_v[...], 0.0)

    @pl.when(first_layer)
    def _():
        keep(along, re, 0.5 * coup_v[im])
        keep(along, im, -0.5 * coup_v[re])
        for rows, part in zip((re, im), halves(along, adjoint, n)):
            base[rows] += part

    @pl.when(later_layer)
    def _():
        prepare()

    pl.semaphore_wait(
        barrier,
        1
        + far_ok.astype(jnp.int32)
        + near_ok.astype(jnp.int32)
        + (x < layers - 1).astype(jnp.int32)
        + sends_twice.astype(jnp.int32),
    )

    def remote(source, target, send_sem, recv_sem, device):
        return pltpu.make_async_remote_copy(
            src_ref=source,
            dst_ref=target,
            send_sem=send_sem,
            recv_sem=recv_sem,
            device_id=device,
            device_id_type=MESH,
        )

    own_half = pl.ds(pl.multiple_of(odd * n, n), n)
    other_half = pl.ds(pl.multiple_of((1 - odd) * n, n), n)

    def constants(i):
        return remote(
            (coup_v, base)[i].at[own_half],
            (again_coup, again_base)[i].at[own_half],
            const_send.at[i],
            const_recv.at[i],
            (layers - 1, m),
        )

    def share(i, half):
        ref = (again_coup, again_base)[i].at[half]
        return remote(ref, ref, share_send.at[i], share_recv.at[i], (x, near))

    def prior_on(t):
        return remote(prior_v.at[t], again_prior.at[t], again_send.at[t], again_recv.at[t], (layers - 1, m))

    @pl.when(constants_on)
    def _():
        constants(0).start()
        constants(1).start()
        for t in range(OWN):
            prior_load(t).wait()
            prior_on(t).start()

    @pl.when(last_layer)
    def _():
        for i in range(2):
            constants(i).wait_recv()
            share(i, own_half).start()
        for i in range(2):
            share(i, other_half).wait_recv()
        factors(again_coup, again_coupled, again_adjoint)

    quarter = n // 2

    def to_next(t, part):
        rows = pl.ds(part * quarter, quarter)
        return pltpu.make_async_remote_copy(
            src_ref=slots.at[7 + t, rows],
            dst_ref=inc.at[t, rows],
            send_sem=xs_sem.at[t, part],
            recv_sem=xr_sem.at[t, part],
            device_id=(jnp.minimum(x + 1, layers - 1), m),
            device_id_type=MESH,
        )

    def to_last(t, part):
        rows = pl.ds(part * quarter, quarter)
        return remote(
            slots.at[7 + t, rows],
            inc.at[t, rows],
            twice_sem.at[t, part],
            xr_sem.at[t, part],
            (layers - 1, m),
        )

    def send(source, target, send_sem, device):
        return pltpu.make_async_remote_copy(
            src_ref=slots.at[source],
            dst_ref=slots.at[target],
            send_sem=send_sem,
            recv_sem=slot_sem.at[target],
            device_id=(x, device),
            device_id_type=MESH,
        )

    def to_near(t):
        return send(7 + t, 14 - t, near_sem.at[t], near)

    def to_far(t):
        return send(7 + t, 6 - t, far_sem.at[t], far)

    def last_step(part, target, i, device):
        rows = pl.ds(part * quarter, quarter)
        return pltpu.make_async_remote_copy(
            src_ref=slots.at[7 + OWN - 1, rows],
            dst_ref=slots.at[target, rows],
            send_sem=last_send.at[i, part],
            recv_sem=last_recv.at[i, part],
            device_id=(x, device),
            device_id_type=MESH,
        )

    def last_to_far(part):
        return last_step(part, 6 - (OWN - 1), 0, far)

    def last_to_skip(part):
        return last_step(part, OWN - 2, 1, skip)

    def to_skip(t):
        return send(7 + t, t - 1, skip_sem.at[t], skip)

    def forward(t):
        return send(6 - t, 15 + t, fwd_sem.at[t], near)

    def arrived(slot):
        send(slot, slot, near_sem.at[0], near).wait_recv()

    def accumulate(sources, first=0, last=2 * n, final=False):
        taps = [[table[u - v + 3] for v in range(OWN)] for u in sources]

        def body(c, carry):
            rows = pl.ds(pl.multiple_of(c * 16, 16), 16)
            blocks = [slots[u, rows, :] for u in sources]
            for v in range(OWN):
                total = acc[v, rows, :]
                for s in range(len(sources)):
                    total = total + taps[s][v] * blocks[s]
                if final:
                    out[place(v), rows, :] = total
                else:
                    acc[v, rows, :] = total
            return carry

        lax.fori_loop(first // 16, last // 16, body, 0)

    def gather(t):
        @pl.when(far_ok)
        def _():
            arrived(6 - t)
            forward(t).start()

        arrived(14 - t)
        accumulate([7 + t, 14 - t, 6 - t])

        @pl.when(t > 0)
        def _():
            @pl.when(far_ok)
            def _():
                arrived(t - 1)

            @pl.when(near_ok)
            def _():
                arrived(14 + t)

            accumulate([t - 1, 14 + t])

    def reciprocal(diag_real, diag_imag):
        modulus = diag_real * diag_real + diag_imag * diag_imag
        columns = diag_real / modulus, -diag_imag / modulus
        return [
            (column, jnp.sum(jnp.where(eye, column, 0.0), axis=0, keepdims=True))
            for column in columns
        ]

    def start_sweeps(q, size, real, imag, inverse):
        rows = slice(q * size, (q + 1) * size)
        (col_real, row_real), (col_imag, row_imag) = inverse
        on = eye[rows]
        real, imag = jnp.where(on, 0.0, real), jnp.where(on, 0.0, imag)
        res_real = real * row_real - imag * row_imag
        res_imag = real * row_imag + imag * row_real
        keep(residue, rows, res_real)
        keep(residue, slice(n + q * size, n + (q + 1) * size), res_imag)
        cr, ci = col_real[rows], col_imag[rows]
        one[q * size : (q + 1) * size] = jnp.where(on, row_real, cr * res_real - ci * res_imag)
        one[n + q * size : n + (q + 1) * size] = jnp.where(on, row_imag, cr * res_imag + ci * res_real)

    def diagonal(level):
        return (
            jnp.sum(jnp.where(eye, level - contact[re], 0.0), axis=1, keepdims=True),
            jnp.sum(jnp.where(eye, -contact[im], 0.0), axis=1, keepdims=True),
        )

    def meet(arriving, wait, left_pair, right_pair, coup_ref, diag):
        diag_real, diag_imag = diag
        wait(0, 1)
        (ch, cl), (in_h, in_l) = left_pair, fourth
        keep(fourth, re, arriving[re])
        left = dot(ch[...], in_h[re]) + (dot(cl[...], in_h[re]) + dot(ch[...], in_l[re]))
        wait(2, 3)
        keep(fourth, im, arriving[im])
        size = n // 2
        diagonals = []
        for q in range(2):
            top, low = slice(q * size, (q + 1) * size), slice(n + q * size, n + (q + 1) * size)

            def right(rows):
                return dot(ch[rows], in_h[im]) + (dot(cl[rows], in_h[im]) + dot(ch[rows], in_l[im]))

            way_real, way_imag = left[top] - right(low), left[low] + right(top)
            keep(along, top, way_real)
            keep(along, low, way_imag)
            diagonals.append(
                (
                    jnp.sum(way_real * coup_ref[top] + way_imag * coup_ref[low], axis=1, keepdims=True),
                    jnp.sum(way_imag * coup_ref[top] - way_real * coup_ref[low], axis=1, keepdims=True),
                )
            )
        on_real, on_imag = (jnp.concatenate([d[i] for d in diagonals]) for i in range(2))
        inverse = reciprocal(diag_real - on_real, diag_imag - on_imag)
        for q, (top, low, real, imag) in enumerate(row_chunks(along, right_pair, n)):
            start_sweeps(q, size, real + contact[top], imag + contact[low], inverse)

    def sweeps():
        for top, low, real, imag in row_chunks(residue, residue, n):
            keep(square, top, real)
            keep(square, low, imag)
        for top, low, real, imag in row_chunks(square, square, n):
            keep(fourth, top, real)
            keep(fourth, low, imag)
        for rows in (re, im):
            keep(first_sum, rows, one[rows])
        for top, low, real, imag in row_chunks(first_sum, square, n):
            two[top] = one[top] + real
            two[low] = one[low] + imag
            keep(second_sum, top, two[top])
            keep(second_sum, low, two[low])
        for top, low, real, imag in row_chunks(second_sum, fourth, n):
            yield top, low, two[top] + real, two[low] + imag

    def step(t, carry):
        @pl.when(jnp.logical_not(constants_on))
        def _():
            prior_load(t).wait()

        energy = (m * OWN + place(t)).astype(F32)
        level = -1.0 + 2.0 * (energy + 0.5) / (groups * OWN)

        def come(*parts):
            for p in parts:
                to_next(t, p).wait_recv()

        @pl.when(last_layer)
        def _():
            prior_on(t).wait_recv()
            contact[...] = again_base[...] + again_prior[t]
            meet(inc.at[t], come, again_coupled, again_adjoint, again_coup, diagonal(level))
            for top, low, real, imag in sweeps():
                inc[t, top] = real
                inc[t, low] = imag

        contact[...] = base[...] + prior_v[t]
        diag = diagonal(level)

        @pl.when(first_layer)
        def _():
            start_sweeps(0, n, contact[re], contact[im], reciprocal(*diag))

        def come_here(*parts):
            @pl.when(jnp.logical_not(last_layer))
            def _():
                come(*parts)

        @pl.when(later_layer)
        def _():
            meet(inc.at[t], come_here, coupled, adjoint, coup_v, diag)

        at_once = jnp.logical_and(has_next, jnp.logical_or(later_layer, t + odd == 0))
        for q, (top, low, real, imag) in enumerate(sweeps()):
            slots[7 + t, top] = real
            slots[7 + t, low] = imag

            @pl.when(at_once)
            def _():
                to_next(t, q).start()
                to_next(t, 2 + q).start()

            @pl.when(sends_twice)
            def _():
                to_last(t, q).start()
                to_last(t, 2 + q).start()

            @pl.when(jnp.logical_and(far_ok, t == OWN - 1))
            def _():
                last_to_far(q).start()
                last_to_far(2 + q).start()

            @pl.when(jnp.logical_and(near_ok, t == OWN - 1))
            def _():
                last_to_skip(q).start()
                last_to_skip(2 + q).start()

        @pl.when(jnp.logical_and(far_ok, t < OWN - 1))
        def _():
            to_far(t).start()

        @pl.when(jnp.logical_and(near_ok, jnp.logical_and(t > 0, t < OWN - 1)))
        def _():
            to_skip(t).start()

        to_near(t).start()

        @pl.when(jnp.logical_and(first_layer, t + odd > 0))
        def _():
            pl.semaphore_wait(token, 1)
            for p in range(4):
                to_next(t, p).start()

        @pl.when(jnp.logical_and(first_layer, t == 0))
        def _():
            prepare()

        @pl.when(t > 0)
        def _():
            gather(t - 1)

        @pl.when(first_layer)
        def _():
            for p in range(3):
                to_next(t, p).wait_send()

            @pl.when(jnp.logical_or(odd == 0, t < OWN - 1))
            def _():
                pl.semaphore_signal(token, inc=1, device_id=(x, near), device_id_type=MESH)

        return carry

    lax.fori_loop(0, OWN, step, 0)
    t = OWN - 1
    @pl.when(near_ok)
    def _():
        arrived(14 + t)

    arrived(14 - t)
    accumulate([14 + t, 7 + t, 14 - t])
    for part in (0, 2, 1, 3):

        @pl.when(far_ok)
        def _():
            last_to_far(part).wait_recv()
            last_to_skip(part).wait_recv()

        accumulate([6 - t, t - 1], part * quarter, (part + 1) * quarter, final=True)
    for i in range(2):

        @pl.when(constants_on)
        def _():
            constants(i).wait_send()

        @pl.when(last_layer)
        def _():
            share(i, own_half).wait_send()

    for t in range(OWN):
        to_near(t).wait_send()

        @pl.when(has_next)
        def _():
            @pl.when(later_layer)
            def _():
                for p in range(3):
                    to_next(t, p).wait_send()

            to_next(t, 3).wait_send()

        @pl.when(sends_twice)
        def _():
            for p in range(4):
                to_last(t, p).wait_send()

        @pl.when(constants_on)
        def _():
            prior_on(t).wait_send()

        @pl.when(far_ok)
        def _():
            if t < OWN - 1:
                to_far(t).wait_send()
                forward(t).wait_send()
            else:
                for part in range(4):
                    last_to_far(part).wait_send()

        if t > 0:

            @pl.when(near_ok)
            def _():
                if t < OWN - 1:
                    to_skip(t).wait_send()
                else:
                    for part in range(4):
                        last_to_skip(part).wait_send()


def solution(mesh):
    layers, groups = mesh.shape["layer"], mesh.shape["energy"]

    def local(onsite, broad, ham, coup, mask, prior, weights, offsets):
        n = onsite.shape[-1]
        hbm = pl.BlockSpec(memory_space=pltpu.HBM)
        block = (2 * n, n)
        result = pl.pallas_call(
            functools.partial(kernel, layers, groups),
            out_shape=jax.ShapeDtypeStruct((OWN, 2 * n, n), F32),
            in_specs=[hbm] * 8,
            out_specs=pl.BlockSpec(memory_space=pltpu.VMEM),
            scratch_shapes=[
                pltpu.VMEM((1, n), F32),
                pltpu.VMEM((1, n), F32),
                pltpu.SMEM((TAPS,), F32),
                pltpu.SMEM((TAPS,), jnp.int32),
                pltpu.VMEM((OWN, *block), F32),
                pltpu.VMEM(block, F32),
                pltpu.VMEM(block, F32),
                pltpu.VMEM((n, n), jnp.int32),
                pltpu.VMEM((SLOTS, *block), F32),
                pltpu.VMEM((OWN, *block), F32),
                pltpu.VMEM((OWN, *block), F32),
                pltpu.VMEM(block, F32),
                pltpu.VMEM(block, F32),
                pltpu.VMEM(block, F32),
                pltpu.VMEM(block, F32),
                pltpu.VMEM(block, F32),
                pltpu.VMEM(block, F32),
                pltpu.VMEM((OWN, *block), F32),
                pltpu.VMEM((20, *block), BF16),
                pltpu.SMEM((SLOTS + 3,), F32),
                pltpu.SemaphoreType.DMA((7,)),
                pltpu.SemaphoreType.DMA((OWN,)),
                pltpu.SemaphoreType.DMA((OWN, 4)),
                pltpu.SemaphoreType.DMA((OWN, 4)),
                pltpu.SemaphoreType.DMA((OWN,)),
                pltpu.SemaphoreType.DMA((OWN,)),
                pltpu.SemaphoreType.DMA((OWN,)),
                pltpu.SemaphoreType.DMA((OWN,)),
                pltpu.SemaphoreType.DMA((SLOTS,)),
                pltpu.SemaphoreType.DMA((2, 4)),
                pltpu.SemaphoreType.DMA((2, 4)),
                pltpu.SemaphoreType.DMA((OWN, 4)),
                pltpu.SemaphoreType.DMA((2,)),
                pltpu.SemaphoreType.DMA((2,)),
                pltpu.SemaphoreType.DMA((2,)),
                pltpu.SemaphoreType.DMA((2,)),
                pltpu.SemaphoreType.DMA((OWN,)),
                pltpu.SemaphoreType.DMA((OWN,)),
                pltpu.SemaphoreType.REGULAR,
            ],
            compiler_params=pltpu.CompilerParams(
                collective_id=0, has_side_effects=True, vmem_limit_bytes=50 * 2**20
            ),
        )(
            *(
                pltpu.with_memory_space_constraint(v, pltpu.HBM)
                for v in (
                    onsite,
                    broad,
                    weights,
                    offsets,
                    ham.reshape(block),
                    coup.reshape(block),
                    mask.reshape(n, n),
                    prior.reshape(OWN, *block),
                )
            ),
        )
        return result.reshape(1, OWN, 2, n, n)

    return jax.shard_map(
        local,
        mesh=mesh,
        in_specs=(
            P("layer", None),
            P("layer", None),
            P("layer", None, None, None),
            P("layer", None, None, None),
            P("layer", None, None),
            P("layer", "energy", None, None, None),
            P(),
            P(),
        ),
        out_specs=P("layer", "energy", None, None, None),
        check_vma=False,
    )
```

```python
import functools

import jax
import jax.numpy as jnp
from jax import lax
from jax.experimental import pallas as pl
from jax.experimental.pallas import tpu as pltpu
from jax.sharding import PartitionSpec as P

MESH = pl.DeviceIdType.MESH
F32 = jnp.float32
BF16 = jnp.bfloat16
OWN = 4
SLOTS = 18
TAPS = 8


def split(value):
    high = value.astype(BF16)
    low = (value - high.astype(F32)).astype(BF16)
    return high, low


def dot(a, b):
    return jnp.dot(a, b, preferred_element_type=F32)


def halves(first, second, n):
    fh, fl = first
    sh, sl = second
    re, im = slice(0, n), slice(n, 2 * n)

    def three(rows, part):
        return dot(fh[rows], sh[part]) + (dot(fl[rows], sh[part]) + dot(fh[rows], sl[part]))

    yield three(re, re) - three(im, im)
    yield three(im, re) + three(re, im)


def row_chunks(first, second, n, count=2):
    fh, fl = first
    sh, sl = second
    re, im = slice(0, n), slice(n, 2 * n)

    def three(rows, part):
        return dot(fh[rows], sh[part]) + (dot(fl[rows], sh[part]) + dot(fh[rows], sl[part]))

    size = n // count
    for q in range(count):
        top, low = slice(q * size, (q + 1) * size), slice(n + q * size, n + (q + 1) * size)
        yield top, low, three(top, re) - three(low, im), three(low, re) + three(top, im)


def kernel(
    layers,
    groups,
    onsite,
    broad,
    weights,
    offsets,
    ham,
    coup,
    mask,
    prior,
    out,
    onsite_v,
    broad_v,
    weights_s,
    offsets_s,
    prior_v,
    ham_v,
    coup_v,
    mask_v,
    slots,
    inc,
    acc,
    base,
    contact,
    one,
    two,
    again_coup,
    again_prior,
    pairs,
    table,
    load_sem,
    prior_sem,
    xs_sem,
    xr_sem,
    near_sem,
    far_sem,
    skip_sem,
    fwd_sem,
    slot_sem,
    last_send,
    last_recv,
    twice_sem,
    const_send,
    const_recv,
    share_send,
    share_recv,
    again_send,
    again_recv,
    token,
):
    n = onsite.shape[-1]
    x = lax.axis_index("layer")
    m = lax.axis_index("energy")
    odd = lax.rem(m, 2)
    sign = 1 - 2 * odd
    near = m + sign
    far = m - sign
    skip = m + 2 * sign
    behind = m - 2 * sign
    near_ok = jnp.logical_and(skip >= 0, skip < groups)
    far_ok = jnp.logical_and(far >= 0, far < groups)
    first_layer = x == 0
    later_layer = x > 0
    has_next = x < layers - 2
    sends_twice = x == layers - 3
    constants_on = x == layers - 2
    last_layer = x == layers - 1
    re, im = slice(0, n), slice(n, 2 * n)
    coupled, adjoint, along, residue, square, first_sum, fourth, second_sum = (
        (pairs.at[2 * i], pairs.at[2 * i + 1]) for i in range(8)
    )
    again_coupled, again_adjoint = ((pairs.at[2 * i], pairs.at[2 * i + 1]) for i in (8, 9))

    def keep(pair, rows, value):
        pair[0][rows], pair[1][rows] = split(value)

    def place(t):
        return jnp.where(odd == 1, OWN - 1 - t, t)

    def prior_load(t):
        return pltpu.make_async_copy(prior.at[place(t)], prior_v.at[t], prior_sem.at[t])

    loads = [
        pltpu.make_async_copy(source, target, load_sem.at[i])
        for i, (source, target) in enumerate(
            [
                (coup, coup_v),
                (mask, mask_v),
                (ham, ham_v),
                (onsite, onsite_v),
                (broad, broad_v),
                (weights, weights_s),
                (offsets, offsets_s),
            ]
        )
    ]
    for load in loads[:3]:
        load.start()
    prior_load(0).start()
    for load in loads[3:]:
        load.start()
    for t in range(1, OWN):
        prior_load(t).start()

    barrier = pltpu.get_barrier_semaphore()
    pl.semaphore_signal(barrier, inc=1, device_id=(x, near), device_id_type=MESH)

    @pl.when(far_ok)
    def _():
        pl.semaphore_signal(barrier, inc=1, device_id=(x, far), device_id_type=MESH)
        pl.semaphore_signal(barrier, inc=1, device_id=(x, behind), device_id_type=MESH)

    @pl.when(later_layer)
    def _():
        pl.semaphore_signal(barrier, inc=1, device_id=(x - 1, m), device_id_type=MESH)

    @pl.when(last_layer)
    def _():
        pl.semaphore_signal(barrier, inc=1, device_id=(layers - 3, m), device_id_type=MESH)

    def prepare():
        acc[...] = jnp.zeros_like(acc)

        @pl.when(jnp.logical_not(far_ok))
        def _():
            slots[0:7] = jnp.zeros((7, 2 * n, n), F32)

        @pl.when(jnp.logical_not(near_ok))
        def _():
            slots[15:18] = jnp.zeros((3, 2 * n, n), F32)

        loads[5].wait()
        loads[6].wait()
        for i in range(SLOTS + 3):
            tap = F32(0.0)
            for j in range(TAPS):
                tap = tap + jnp.where(offsets_s[j] * sign == i - 10, weights_s[j], F32(0.0))
            table[i] = tap

    loads[0].wait()
    loads[1].wait()
    kept = mask_v[...].astype(F32)
    coup_v[re] = coup_v[re] * kept
    coup_v[im] = coup_v[im] * kept

    def factors(source, left, right):
        keep(left, re, source[re])
        keep(left, im, source[im])
        keep(right, re, source[re].T)
        keep(right, im, -source[im].T)

    factors(coup_v, coupled, adjoint)
    for load in loads[2:5]:
        load.wait()
    eye = lax.broadcasted_iota(jnp.int32, (n, n), 0) == lax.broadcasted_iota(jnp.int32, (n, n), 1)
    base[re] = 0.5 * (ham_v[re] + ham_v[re].T) + jnp.where(eye, onsite_v[...], 0.0)
    base[im] = 0.5 * (ham_v[im] - ham_v[im].T) - jnp.where(eye, broad_v[...], 0.0)

    @pl.when(first_layer)
    def _():
        keep(along, re, 0.5 * coup_v[im])
        keep(along, im, -0.5 * coup_v[re])
        for rows, part in zip((re, im), halves(along, adjoint, n)):
            base[rows] += part

    @pl.when(later_layer)
    def _():
        prepare()

    pl.semaphore_wait(
        barrier,
        1
        + far_ok.astype(jnp.int32)
        + near_ok.astype(jnp.int32)
        + (x < layers - 1).astype(jnp.int32)
        + sends_twice.astype(jnp.int32),
    )

    def remote(source, target, send_sem, recv_sem, device):
        return pltpu.make_async_remote_copy(
            src_ref=source,
            dst_ref=target,
            send_sem=send_sem,
            recv_sem=recv_sem,
            device_id=device,
            device_id_type=MESH,
        )

    own_half = pl.ds(pl.multiple_of(odd * n, n), n)
    other_half = pl.ds(pl.multiple_of((1 - odd) * n, n), n)

    def constants():
        return remote(coup_v.at[own_half], again_coup.at[own_half], const_send, const_recv, (layers - 1, m))

    def share(half):
        ref = again_coup.at[half]
        return remote(ref, ref, share_send, share_recv, (x, near))

    def prior_on(t):
        return remote(prior_v.at[t], again_prior.at[t], again_send.at[t], again_recv.at[t], (layers - 1, m))

    @pl.when(constants_on)
    def _():
        constants().start()
        for t in range(OWN):
            prior_load(t).wait()
            prior_v[t] = prior_v[t] + base[...]
        constants().wait_send()
        prior_on(0).start()
        prior_on(0).wait_send()
        prior_on(1).start()

    @pl.when(last_layer)
    def _():
        constants().wait_recv()
        share(own_half).start()
        share(other_half).wait_recv()
        factors(again_coup, again_coupled, again_adjoint)

    quarter = n // 2

    def to_next(t, part):
        rows = pl.ds(part * quarter, quarter)
        return pltpu.make_async_remote_copy(
            src_ref=slots.at[7 + t, rows],
            dst_ref=inc.at[t, rows],
            send_sem=xs_sem.at[t, part],
            recv_sem=xr_sem.at[t, part],
            device_id=(jnp.minimum(x + 1, layers - 1), m),
            device_id_type=MESH,
        )

    def to_last(t, part):
        rows = pl.ds(part * quarter, quarter)
        return remote(
            slots.at[7 + t, rows],
            inc.at[t, rows],
            twice_sem.at[t, part],
            xr_sem.at[t, part],
            (layers - 1, m),
        )

    def send(source, target, send_sem, device):
        return pltpu.make_async_remote_copy(
            src_ref=slots.at[source],
            dst_ref=slots.at[target],
            send_sem=send_sem,
            recv_sem=slot_sem.at[target],
            device_id=(x, device),
            device_id_type=MESH,
        )

    def to_near(t):
        return send(7 + t, 14 - t, near_sem.at[t], near)

    def to_far(t):
        return send(7 + t, 6 - t, far_sem.at[t], far)

    def last_step(part, target, i, device):
        rows = pl.ds(part * quarter, quarter)
        return pltpu.make_async_remote_copy(
            src_ref=slots.at[7 + OWN - 1, rows],
            dst_ref=slots.at[target, rows],
            send_sem=last_send.at[i, part],
            recv_sem=last_recv.at[i, part],
            device_id=(x, device),
            device_id_type=MESH,
        )

    def last_to_far(part):
        return last_step(part, 6 - (OWN - 1), 0, far)

    def last_to_skip(part):
        return last_step(part, OWN - 2, 1, skip)

    def to_skip(t):
        return send(7 + t, t - 1, skip_sem.at[t], skip)

    def forward(t):
        return send(6 - t, 15 + t, fwd_sem.at[t], near)

    def arrived(slot):
        send(slot, slot, near_sem.at[0], near).wait_recv()

    def accumulate(sources, first=0, last=2 * n, final=False):
        taps = [[table[u - v + 3] for v in range(OWN)] for u in sources]

        def body(c, carry):
            rows = pl.ds(pl.multiple_of(c * 16, 16), 16)
            blocks = [slots[u, rows, :] for u in sources]
            for v in range(OWN):
                total = acc[v, rows, :]
                for s in range(len(sources)):
                    total = total + taps[s][v] * blocks[s]
                if final:
                    out[place(v), rows, :] = total
                else:
                    acc[v, rows, :] = total
            return carry

        lax.fori_loop(first // 16, last // 16, body, 0)

    def gather(t):
        @pl.when(far_ok)
        def _():
            arrived(6 - t)
            forward(t).start()

        arrived(14 - t)
        accumulate([7 + t, 14 - t, 6 - t])

        @pl.when(t > 0)
        def _():
            @pl.when(far_ok)
            def _():
                arrived(t - 1)

            @pl.when(near_ok)
            def _():
                arrived(14 + t)

            accumulate([t - 1, 14 + t])

    def reciprocal(diag_real, diag_imag):
        modulus = diag_real * diag_real + diag_imag * diag_imag
        columns = diag_real / modulus, -diag_imag / modulus
        return [
            (column, jnp.sum(jnp.where(eye, column, 0.0), axis=0, keepdims=True))
            for column in columns
        ]

    def start_sweeps(q, size, real, imag, inverse):
        rows = slice(q * size, (q + 1) * size)
        (col_real, row_real), (col_imag, row_imag) = inverse
        on = eye[rows]
        real, imag = jnp.where(on, 0.0, real), jnp.where(on, 0.0, imag)
        res_real = real * row_real - imag * row_imag
        res_imag = real * row_imag + imag * row_real
        keep(residue, rows, res_real)
        keep(residue, slice(n + q * size, n + (q + 1) * size), res_imag)
        cr, ci = col_real[rows], col_imag[rows]
        one_real = jnp.where(on, row_real, cr * res_real - ci * res_imag)
        one_imag = jnp.where(on, row_imag, cr * res_imag + ci * res_real)
        low = slice(n + q * size, n + (q + 1) * size)
        one[rows], one[low] = one_real, one_imag
        keep(first_sum, rows, one_real)
        keep(first_sum, low, one_imag)

    def diagonal(level):
        return (
            jnp.sum(jnp.where(eye, level - contact[re], 0.0), axis=1, keepdims=True),
            jnp.sum(jnp.where(eye, -contact[im], 0.0), axis=1, keepdims=True),
        )

    def meet(arriving, wait, left_pair, right_pair, coup_ref, diag):
        diag_real, diag_imag = diag
        wait(0, 1)
        (ch, cl), (in_h, in_l) = left_pair, fourth
        keep(fourth, re, arriving[re])
        left = dot(ch[...], in_h[re]) + (dot(cl[...], in_h[re]) + dot(ch[...], in_l[re]))
        wait(2, 3)
        keep(fourth, im, arriving[im])
        size = n // 2
        diagonals = []
        for q in range(2):
            top, low = slice(q * size, (q + 1) * size), slice(n + q * size, n + (q + 1) * size)

            def right(rows):
                return dot(ch[rows], in_h[im]) + (dot(cl[rows], in_h[im]) + dot(ch[rows], in_l[im]))

            way_real, way_imag = left[top] - right(low), left[low] + right(top)
            keep(along, top, way_real)
            keep(along, low, way_imag)
            diagonals.append(
                (
                    jnp.sum(way_real * coup_ref[top] + way_imag * coup_ref[low], axis=1, keepdims=True),
                    jnp.sum(way_imag * coup_ref[top] - way_real * coup_ref[low], axis=1, keepdims=True),
                )
            )
        on_real, on_imag = (jnp.concatenate([d[i] for d in diagonals]) for i in range(2))
        inverse = reciprocal(diag_real - on_real, diag_imag - on_imag)
        for q, (top, low, real, imag) in enumerate(row_chunks(along, right_pair, n)):
            start_sweeps(q, size, real + contact[top], imag + contact[low], inverse)

    def sweeps():
        for top, low, real, imag in row_chunks(residue, residue, n):
            keep(square, top, real)
            keep(square, low, imag)
        for top, low, real, imag in row_chunks(square, square, n):
            keep(fourth, top, real)
            keep(fourth, low, imag)
        for top, low, real, imag in row_chunks(first_sum, square, n):
            two[top] = one[top] + real
            two[low] = one[low] + imag
            keep(second_sum, top, two[top])
            keep(second_sum, low, two[low])
        for top, low, real, imag in row_chunks(second_sum, fourth, n):
            yield top, low, two[top] + real, two[low] + imag

    def step(t, carry):
        @pl.when(jnp.logical_not(constants_on))
        def _():
            prior_load(t).wait()

        energy = (m * OWN + place(t)).astype(F32)
        level = -1.0 + 2.0 * (energy + 0.5) / (groups * OWN)

        def come(*parts):
            for p in parts:
                to_next(t, p).wait_recv()

        @pl.when(last_layer)
        def _():
            prior_on(t).wait_recv()
            contact[...] = again_prior[t]
            meet(inc.at[t], come, again_coupled, again_adjoint, again_coup, diagonal(level))
            for top, low, real, imag in sweeps():
                inc[t, top] = real
                inc[t, low] = imag

        @pl.when(constants_on)
        def _():
            contact[...] = prior_v[t]

        @pl.when(jnp.logical_not(constants_on))
        def _():
            contact[...] = base[...] + prior_v[t]

        diag = diagonal(level)

        @pl.when(first_layer)
        def _():
            start_sweeps(0, n, contact[re], contact[im], reciprocal(*diag))

        def come_here(*parts):
            @pl.when(jnp.logical_not(last_layer))
            def _():
                come(*parts)

        @pl.when(later_layer)
        def _():
            meet(inc.at[t], come_here, coupled, adjoint, coup_v, diag)

        at_once = jnp.logical_and(has_next, jnp.logical_or(later_layer, t + odd == 0))
        for q, (top, low, real, imag) in enumerate(sweeps()):
            slots[7 + t, top] = real
            slots[7 + t, low] = imag

            @pl.when(sends_twice)
            def _():
                to_last(t, q).start()
                to_last(t, 2 + q).start()

            @pl.when(at_once)
            def _():
                to_next(t, q).start()
                to_next(t, 2 + q).start()

            @pl.when(jnp.logical_and(far_ok, t == OWN - 1))
            def _():
                last_to_far(q).start()
                last_to_far(2 + q).start()

            @pl.when(jnp.logical_and(near_ok, t == OWN - 1))
            def _():
                last_to_skip(q).start()
                last_to_skip(2 + q).start()

        @pl.when(jnp.logical_and(far_ok, t < OWN - 1))
        def _():
            to_far(t).start()

        @pl.when(jnp.logical_and(near_ok, jnp.logical_and(t > 0, t < OWN - 1)))
        def _():
            to_skip(t).start()

        to_near(t).start()

        @pl.when(jnp.logical_and(constants_on, t < OWN - 2))
        def _():
            prior_on(t + 1).wait_send()
            prior_on(t + 2).start()

        @pl.when(jnp.logical_and(first_layer, t + odd > 0))
        def _():
            pl.semaphore_wait(token, 1)
            for p in range(4):
                to_next(t, p).start()

        @pl.when(jnp.logical_and(first_layer, t == 0))
        def _():
            prepare()

        @pl.when(t > 0)
        def _():
            gather(t - 1)

        @pl.when(first_layer)
        def _():
            for p in range(3):
                to_next(t, p).wait_send()

            @pl.when(jnp.logical_or(odd == 0, t < OWN - 1))
            def _():
                pl.semaphore_signal(token, inc=1, device_id=(x, near), device_id_type=MESH)

        return carry

    lax.fori_loop(0, OWN, step, 0)
    t = OWN - 1
    @pl.when(near_ok)
    def _():
        arrived(14 + t)

    arrived(14 - t)
    accumulate([14 + t, 7 + t, 14 - t])
    for part in (0, 2, 1, 3):

        @pl.when(far_ok)
        def _():
            last_to_far(part).wait_recv()
            last_to_skip(part).wait_recv()

        accumulate([6 - t, t - 1], part * quarter, (part + 1) * quarter, final=True)
    @pl.when(constants_on)
    def _():
        prior_on(OWN - 1).wait_send()

    @pl.when(last_layer)
    def _():
        share(own_half).wait_send()

    for t in range(OWN):
        to_near(t).wait_send()

        @pl.when(has_next)
        def _():
            @pl.when(later_layer)
            def _():
                for p in range(3):
                    to_next(t, p).wait_send()

            to_next(t, 3).wait_send()

        @pl.when(sends_twice)
        def _():
            for p in range(4):
                to_last(t, p).wait_send()

        @pl.when(far_ok)
        def _():
            if t < OWN - 1:
                to_far(t).wait_send()
                forward(t).wait_send()
            else:
                for part in range(4):
                    last_to_far(part).wait_send()

        if t > 0:

            @pl.when(near_ok)
            def _():
                if t < OWN - 1:
                    to_skip(t).wait_send()
                else:
                    for part in range(4):
                        last_to_skip(part).wait_send()


def solution(mesh):
    layers, groups = mesh.shape["layer"], mesh.shape["energy"]

    def local(onsite, broad, ham, coup, mask, prior, weights, offsets):
        n = onsite.shape[-1]
        hbm = pl.BlockSpec(memory_space=pltpu.HBM)
        block = (2 * n, n)
        result = pl.pallas_call(
            functools.partial(kernel, layers, groups),
            out_shape=jax.ShapeDtypeStruct((OWN, 2 * n, n), F32),
            in_specs=[hbm] * 8,
            out_specs=pl.BlockSpec(memory_space=pltpu.VMEM),
            scratch_shapes=[
                pltpu.VMEM((1, n), F32),
                pltpu.VMEM((1, n), F32),
                pltpu.SMEM((TAPS,), F32),
                pltpu.SMEM((TAPS,), jnp.int32),
                pltpu.VMEM((OWN, *block), F32),
                pltpu.VMEM(block, F32),
                pltpu.VMEM(block, F32),
                pltpu.VMEM((n, n), jnp.int32),
                pltpu.VMEM((SLOTS, *block), F32),
                pltpu.VMEM((OWN, *block), F32),
                pltpu.VMEM((OWN, *block), F32),
                pltpu.VMEM(block, F32),
                pltpu.VMEM(block, F32),
                pltpu.VMEM(block, F32),
                pltpu.VMEM(block, F32),
                pltpu.VMEM(block, F32),
                pltpu.VMEM((OWN, *block), F32),
                pltpu.VMEM((20, *block), BF16),
                pltpu.SMEM((SLOTS + 3,), F32),
                pltpu.SemaphoreType.DMA((7,)),
                pltpu.SemaphoreType.DMA((OWN,)),
                pltpu.SemaphoreType.DMA((OWN, 4)),
                pltpu.SemaphoreType.DMA((OWN, 4)),
                pltpu.SemaphoreType.DMA((OWN,)),
                pltpu.SemaphoreType.DMA((OWN,)),
                pltpu.SemaphoreType.DMA((OWN,)),
                pltpu.SemaphoreType.DMA((OWN,)),
                pltpu.SemaphoreType.DMA((SLOTS,)),
                pltpu.SemaphoreType.DMA((2, 4)),
                pltpu.SemaphoreType.DMA((2, 4)),
                pltpu.SemaphoreType.DMA((OWN, 4)),
                pltpu.SemaphoreType.DMA,
                pltpu.SemaphoreType.DMA,
                pltpu.SemaphoreType.DMA,
                pltpu.SemaphoreType.DMA,
                pltpu.SemaphoreType.DMA((OWN,)),
                pltpu.SemaphoreType.DMA((OWN,)),
                pltpu.SemaphoreType.REGULAR,
            ],
            compiler_params=pltpu.CompilerParams(
                collective_id=0, has_side_effects=True, vmem_limit_bytes=50 * 2**20
            ),
        )(
            *(
                pltpu.with_memory_space_constraint(v, pltpu.HBM)
                for v in (
                    onsite,
                    broad,
                    weights,
                    offsets,
                    ham.reshape(block),
                    coup.reshape(block),
                    mask.reshape(n, n),
                    prior.reshape(OWN, *block),
                )
            ),
        )
        return result.reshape(1, OWN, 2, n, n)

    return jax.shard_map(
        local,
        mesh=mesh,
        in_specs=(
            P("layer", None),
            P("layer", None),
            P("layer", None, None, None),
            P("layer", None, None, None),
            P("layer", None, None),
            P("layer", "energy", None, None, None),
            P(),
            P(),
        ),
        out_specs=P("layer", "energy", None, None, None),
        check_vma=False,
    )
```

```python
import functools

import jax
import jax.numpy as jnp
from jax import lax
from jax.experimental import pallas as pl
from jax.experimental.pallas import tpu as pltpu
from jax.sharding import PartitionSpec as P

MESH = pl.DeviceIdType.MESH
F32 = jnp.float32
BF16 = jnp.bfloat16
OWN = 4
SLOTS = 18
TAPS = 8


def split(value):
    high = value.astype(BF16)
    low = (value - high.astype(F32)).astype(BF16)
    return high, low


def dot(a, b):
    return jnp.dot(a, b, preferred_element_type=F32)


def halves(first, second, n):
    fh, fl = first
    sh, sl = second
    re, im = slice(0, n), slice(n, 2 * n)

    def three(rows, part):
        return dot(fh[rows], sh[part]) + (dot(fl[rows], sh[part]) + dot(fh[rows], sl[part]))

    yield three(re, re) - three(im, im)
    yield three(im, re) + three(re, im)


def row_chunks(first, second, n, count=2):
    fh, fl = first
    sh, sl = second
    re, im = slice(0, n), slice(n, 2 * n)

    def three(rows, part):
        return dot(fh[rows], sh[part]) + (dot(fl[rows], sh[part]) + dot(fh[rows], sl[part]))

    size = n // count
    for q in range(count):
        top, low = slice(q * size, (q + 1) * size), slice(n + q * size, n + (q + 1) * size)
        yield top, low, three(top, re) - three(low, im), three(low, re) + three(top, im)


def kernel(
    layers,
    groups,
    onsite,
    broad,
    weights,
    offsets,
    ham,
    coup,
    mask,
    prior,
    out,
    onsite_v,
    broad_v,
    weights_s,
    offsets_s,
    prior_v,
    ham_v,
    coup_v,
    mask_v,
    slots,
    inc,
    acc,
    base,
    contact,
    one,
    two,
    again_coup,
    again_prior,
    pairs,
    table,
    load_sem,
    prior_sem,
    xs_sem,
    xr_sem,
    near_sem,
    far_sem,
    skip_sem,
    fwd_sem,
    slot_sem,
    last_send,
    last_recv,
    twice_sem,
    const_send,
    const_recv,
    share_send,
    share_recv,
    again_send,
    again_recv,
    token,
):
    n = onsite.shape[-1]
    x = lax.axis_index("layer")
    m = lax.axis_index("energy")
    odd = lax.rem(m, 2)
    sign = 1 - 2 * odd
    near = m + sign
    far = m - sign
    skip = m + 2 * sign
    behind = m - 2 * sign
    near_ok = jnp.logical_and(skip >= 0, skip < groups)
    far_ok = jnp.logical_and(far >= 0, far < groups)
    first_layer = x == 0
    later_layer = x > 0
    has_next = x < layers - 2
    sends_twice = x == layers - 3
    constants_on = x == layers - 2
    last_layer = x == layers - 1
    re, im = slice(0, n), slice(n, 2 * n)
    coupled, adjoint, along, residue, square, first_sum, fourth, second_sum = (
        (pairs.at[2 * i], pairs.at[2 * i + 1]) for i in range(8)
    )
    again_coupled, again_adjoint = ((pairs.at[2 * i], pairs.at[2 * i + 1]) for i in (8, 9))

    def keep(pair, rows, value):
        pair[0][rows], pair[1][rows] = split(value)

    def place(t):
        return jnp.where(odd == 1, OWN - 1 - t, t)

    def prior_load(t):
        return pltpu.make_async_copy(prior.at[place(t)], prior_v.at[t], prior_sem.at[t])

    loads = [
        pltpu.make_async_copy(source, target, load_sem.at[i])
        for i, (source, target) in enumerate(
            [
                (coup, coup_v),
                (mask, mask_v),
                (ham, ham_v),
                (onsite, onsite_v),
                (broad, broad_v),
                (weights, weights_s),
                (offsets, offsets_s),
            ]
        )
    ]
    for load in loads[:3]:
        load.start()
    prior_load(0).start()
    for load in loads[3:]:
        load.start()
    for t in range(1, OWN):
        prior_load(t).start()

    barrier = pltpu.get_barrier_semaphore()
    pl.semaphore_signal(barrier, inc=1, device_id=(x, near), device_id_type=MESH)

    @pl.when(far_ok)
    def _():
        pl.semaphore_signal(barrier, inc=1, device_id=(x, far), device_id_type=MESH)
        pl.semaphore_signal(barrier, inc=1, device_id=(x, behind), device_id_type=MESH)

    @pl.when(later_layer)
    def _():
        pl.semaphore_signal(barrier, inc=1, device_id=(x - 1, m), device_id_type=MESH)

    @pl.when(last_layer)
    def _():
        pl.semaphore_signal(barrier, inc=1, device_id=(layers - 3, m), device_id_type=MESH)

    def prepare():
        acc[...] = jnp.zeros_like(acc)

        @pl.when(jnp.logical_not(far_ok))
        def _():
            slots[0:7] = jnp.zeros((7, 2 * n, n), F32)

        @pl.when(jnp.logical_not(near_ok))
        def _():
            slots[15:18] = jnp.zeros((3, 2 * n, n), F32)

        loads[5].wait()
        loads[6].wait()
        for i in range(SLOTS + 3):
            tap = F32(0.0)
            for j in range(TAPS):
                tap = tap + jnp.where(offsets_s[j] * sign == i - 10, weights_s[j], F32(0.0))
            table[i] = tap

    loads[0].wait()
    loads[1].wait()
    kept = mask_v[...].astype(F32)
    coup_v[re] = coup_v[re] * kept
    coup_v[im] = coup_v[im] * kept

    def factors(source, left, right):
        keep(left, re, source[re])
        keep(left, im, source[im])
        keep(right, re, source[re].T)
        keep(right, im, -source[im].T)

    factors(coup_v, coupled, adjoint)
    for load in loads[2:5]:
        load.wait()
    eye = lax.broadcasted_iota(jnp.int32, (n, n), 0) == lax.broadcasted_iota(jnp.int32, (n, n), 1)
    base[re] = 0.5 * (ham_v[re] + ham_v[re].T) + jnp.where(eye, onsite_v[...], 0.0)
    base[im] = 0.5 * (ham_v[im] - ham_v[im].T) - jnp.where(eye, broad_v[...], 0.0)

    @pl.when(first_layer)
    def _():
        keep(along, re, 0.5 * coup_v[im])
        keep(along, im, -0.5 * coup_v[re])
        for rows, part in zip((re, im), halves(along, adjoint, n)):
            base[rows] += part

    @pl.when(later_layer)
    def _():
        prepare()

    pl.semaphore_wait(
        barrier,
        1
        + far_ok.astype(jnp.int32)
        + near_ok.astype(jnp.int32)
        + (x < layers - 1).astype(jnp.int32)
        + sends_twice.astype(jnp.int32),
    )

    def remote(source, target, send_sem, recv_sem, device):
        return pltpu.make_async_remote_copy(
            src_ref=source,
            dst_ref=target,
            send_sem=send_sem,
            recv_sem=recv_sem,
            device_id=device,
            device_id_type=MESH,
        )

    own_half = pl.ds(pl.multiple_of(odd * n, n), n)
    other_half = pl.ds(pl.multiple_of((1 - odd) * n, n), n)

    def constants():
        return remote(coup_v.at[own_half], again_coup.at[own_half], const_send, const_recv, (layers - 1, m))

    def share(half):
        ref = again_coup.at[half]
        return remote(ref, ref, share_send, share_recv, (x, near))

    def prior_on(t):
        return remote(prior_v.at[t], again_prior.at[t], again_send.at[t], again_recv.at[t], (layers - 1, m))

    @pl.when(constants_on)
    def _():
        constants().start()
        for t in range(OWN):
            prior_load(t).wait()
            prior_v[t] = prior_v[t] + base[...]
        constants().wait_send()
        prior_on(0).start()
        prior_on(0).wait_send()
        prior_on(1).start()

    @pl.when(last_layer)
    def _():
        constants().wait_recv()
        share(own_half).start()
        share(other_half).wait_recv()
        factors(again_coup, again_coupled, again_adjoint)

    quarter = n // 2

    def to_next(t, part):
        rows = pl.ds(part * quarter, quarter)
        return pltpu.make_async_remote_copy(
            src_ref=slots.at[7 + t, rows],
            dst_ref=inc.at[t, rows],
            send_sem=xs_sem.at[t, part],
            recv_sem=xr_sem.at[t, part],
            device_id=(jnp.minimum(x + 1, layers - 1), m),
            device_id_type=MESH,
        )

    def to_last(t, part):
        rows = pl.ds(part * quarter, quarter)
        return remote(
            slots.at[7 + t, rows],
            inc.at[t, rows],
            twice_sem.at[t, part],
            xr_sem.at[t, part],
            (layers - 1, m),
        )

    def send(source, target, send_sem, device):
        return pltpu.make_async_remote_copy(
            src_ref=slots.at[source],
            dst_ref=slots.at[target],
            send_sem=send_sem,
            recv_sem=slot_sem.at[target],
            device_id=(x, device),
            device_id_type=MESH,
        )

    def to_near(t):
        return send(7 + t, 14 - t, near_sem.at[t], near)

    def to_far(t):
        return send(7 + t, 6 - t, far_sem.at[t], far)

    def last_step(part, target, i, device):
        rows = pl.ds(part * quarter, quarter)
        return pltpu.make_async_remote_copy(
            src_ref=slots.at[7 + OWN - 1, rows],
            dst_ref=slots.at[target, rows],
            send_sem=last_send.at[i, part],
            recv_sem=last_recv.at[i, part],
            device_id=(x, device),
            device_id_type=MESH,
        )

    def last_to_far(part):
        return last_step(part, 6 - (OWN - 1), 0, far)

    def last_to_skip(part):
        return last_step(part, OWN - 2, 1, skip)

    def to_skip(t):
        return send(7 + t, t - 1, skip_sem.at[t], skip)

    def forward(t):
        return send(6 - t, 15 + t, fwd_sem.at[t], near)

    def arrived(slot):
        send(slot, slot, near_sem.at[0], near).wait_recv()

    def accumulate(sources, first=0, last=2 * n, final=False):
        taps = [[table[u - v + 3] for v in range(OWN)] for u in sources]

        def body(c, carry):
            rows = pl.ds(pl.multiple_of(c * 16, 16), 16)
            blocks = [slots[u, rows, :] for u in sources]
            for v in range(OWN):
                total = acc[v, rows, :]
                for s in range(len(sources)):
                    total = total + taps[s][v] * blocks[s]
                if final:
                    out[place(v), rows, :] = total
                else:
                    acc[v, rows, :] = total
            return carry

        lax.fori_loop(first // 16, last // 16, body, 0)

    def gather(t):
        @pl.when(far_ok)
        def _():
            arrived(6 - t)
            forward(t).start()

        arrived(14 - t)
        accumulate([7 + t, 14 - t, 6 - t])

        @pl.when(t > 0)
        def _():
            @pl.when(far_ok)
            def _():
                arrived(t - 1)

            @pl.when(near_ok)
            def _():
                arrived(14 + t)

            accumulate([t - 1, 14 + t])

    def reciprocal(diag_real, diag_imag):
        modulus = diag_real * diag_real + diag_imag * diag_imag
        columns = diag_real / modulus, -diag_imag / modulus
        return [
            (column, jnp.sum(jnp.where(eye, column, 0.0), axis=0, keepdims=True))
            for column in columns
        ]

    def start_sweeps(q, size, real, imag, inverse):
        rows = slice(q * size, (q + 1) * size)
        (col_real, row_real), (col_imag, row_imag) = inverse
        on = eye[rows]
        real, imag = jnp.where(on, 0.0, real), jnp.where(on, 0.0, imag)
        res_real = real * row_real - imag * row_imag
        res_imag = real * row_imag + imag * row_real
        keep(residue, rows, res_real)
        keep(residue, slice(n + q * size, n + (q + 1) * size), res_imag)
        cr, ci = col_real[rows], col_imag[rows]
        one_real = jnp.where(on, row_real, cr * res_real - ci * res_imag)
        one_imag = jnp.where(on, row_imag, cr * res_imag + ci * res_real)
        low = slice(n + q * size, n + (q + 1) * size)
        one[rows], one[low] = one_real, one_imag
        keep(first_sum, rows, one_real)
        keep(first_sum, low, one_imag)

    def diagonal(level, rest):
        return (
            jnp.sum(jnp.where(eye, level - rest[re], 0.0), axis=1, keepdims=True),
            jnp.sum(jnp.where(eye, -rest[im], 0.0), axis=1, keepdims=True),
        )

    def meet(arriving, wait, left_pair, right_pair, coup_ref, rest, diag):
        diag_real, diag_imag = diag
        wait(0, 1)
        (ch, cl), (in_h, in_l) = left_pair, fourth
        keep(fourth, re, arriving[re])
        left = dot(ch[...], in_h[re]) + (dot(cl[...], in_h[re]) + dot(ch[...], in_l[re]))
        wait(2, 3)
        keep(fourth, im, arriving[im])
        size = n // 2
        diagonals = []
        for q in range(2):
            top, low = slice(q * size, (q + 1) * size), slice(n + q * size, n + (q + 1) * size)

            def right(rows):
                return dot(ch[rows], in_h[im]) + (dot(cl[rows], in_h[im]) + dot(ch[rows], in_l[im]))

            way_real, way_imag = left[top] - right(low), left[low] + right(top)
            keep(along, top, way_real)
            keep(along, low, way_imag)
            diagonals.append(
                (
                    jnp.sum(way_real * coup_ref[top] + way_imag * coup_ref[low], axis=1, keepdims=True),
                    jnp.sum(way_imag * coup_ref[top] - way_real * coup_ref[low], axis=1, keepdims=True),
                )
            )
        on_real, on_imag = (jnp.concatenate([d[i] for d in diagonals]) for i in range(2))
        inverse = reciprocal(diag_real - on_real, diag_imag - on_imag)
        for q, (top, low, real, imag) in enumerate(row_chunks(along, right_pair, n)):
            start_sweeps(q, size, real + rest[top], imag + rest[low], inverse)

    def sweeps():
        for top, low, real, imag in row_chunks(residue, residue, n):
            keep(square, top, real)
            keep(square, low, imag)
        for top, low, real, imag in row_chunks(square, square, n):
            keep(fourth, top, real)
            keep(fourth, low, imag)
        for top, low, real, imag in row_chunks(first_sum, square, n):
            two[top] = one[top] + real
            two[low] = one[low] + imag
            keep(second_sum, top, two[top])
            keep(second_sum, low, two[low])
        for top, low, real, imag in row_chunks(second_sum, fourth, n):
            yield top, low, two[top] + real, two[low] + imag

    def step(t, carry):
        @pl.when(jnp.logical_not(constants_on))
        def _():
            prior_load(t).wait()

        energy = (m * OWN + place(t)).astype(F32)
        level = -1.0 + 2.0 * (energy + 0.5) / (groups * OWN)

        def come(*parts):
            for p in parts:
                to_next(t, p).wait_recv()

        @pl.when(constants_on)
        def _():
            contact[...] = prior_v[t]

        @pl.when(jnp.logical_not(constants_on))
        def _():
            contact[...] = base[...] + prior_v[t]

        diag = diagonal(level, contact)

        @pl.when(last_layer)
        def _():
            prior_on(t).wait_recv()
            rest = again_prior.at[t]
            meet(inc.at[t], come, again_coupled, again_adjoint, again_coup, rest, diagonal(level, rest))
            for top, low, real, imag in sweeps():
                inc[t, top] = real
                inc[t, low] = imag

        @pl.when(first_layer)
        def _():
            start_sweeps(0, n, contact[re], contact[im], reciprocal(*diag))

        def come_here(*parts):
            @pl.when(jnp.logical_not(last_layer))
            def _():
                come(*parts)

        @pl.when(later_layer)
        def _():
            meet(inc.at[t], come_here, coupled, adjoint, coup_v, contact, diag)

        at_once = jnp.logical_and(has_next, jnp.logical_or(later_layer, t + odd == 0))
        for q, (top, low, real, imag) in enumerate(sweeps()):
            slots[7 + t, top] = real
            slots[7 + t, low] = imag

            @pl.when(sends_twice)
            def _():
                to_last(t, q).start()
                to_last(t, 2 + q).start()

            @pl.when(at_once)
            def _():
                to_next(t, q).start()
                to_next(t, 2 + q).start()

            @pl.when(jnp.logical_and(far_ok, t == OWN - 1))
            def _():
                last_to_far(q).start()
                last_to_far(2 + q).start()

            @pl.when(jnp.logical_and(near_ok, t == OWN - 1))
            def _():
                last_to_skip(q).start()
                last_to_skip(2 + q).start()

        @pl.when(jnp.logical_and(far_ok, t < OWN - 1))
        def _():
            to_far(t).start()

        @pl.when(jnp.logical_and(near_ok, jnp.logical_and(t > 0, t < OWN - 1)))
        def _():
            to_skip(t).start()

        to_near(t).start()

        @pl.when(jnp.logical_and(constants_on, t < OWN - 2))
        def _():
            prior_on(t + 1).wait_send()
            prior_on(t + 2).start()

        @pl.when(jnp.logical_and(first_layer, t + odd > 0))
        def _():
            pl.semaphore_wait(token, 1)
            for p in range(4):
                to_next(t, p).start()

        @pl.when(jnp.logical_and(first_layer, t == 0))
        def _():
            prepare()

        @pl.when(t > 0)
        def _():
            gather(t - 1)

        @pl.when(first_layer)
        def _():
            for p in range(3):
                to_next(t, p).wait_send()

            @pl.when(jnp.logical_or(odd == 0, t < OWN - 1))
            def _():
                pl.semaphore_signal(token, inc=1, device_id=(x, near), device_id_type=MESH)

        return carry

    lax.fori_loop(0, OWN, step, 0)
    t = OWN - 1
    @pl.when(near_ok)
    def _():
        arrived(14 + t)

    arrived(14 - t)
    accumulate([14 + t, 7 + t, 14 - t])
    for part in (0, 2, 1, 3):

        @pl.when(far_ok)
        def _():
            last_to_far(part).wait_recv()
            last_to_skip(part).wait_recv()

        accumulate([6 - t, t - 1], part * quarter, (part + 1) * quarter, final=True)
    @pl.when(constants_on)
    def _():
        prior_on(OWN - 1).wait_send()

    @pl.when(last_layer)
    def _():
        share(own_half).wait_send()

    for t in range(OWN):
        to_near(t).wait_send()

        @pl.when(has_next)
        def _():
            @pl.when(later_layer)
            def _():
                for p in range(3):
                    to_next(t, p).wait_send()

            to_next(t, 3).wait_send()

        @pl.when(sends_twice)
        def _():
            for p in range(4):
                to_last(t, p).wait_send()

        @pl.when(far_ok)
        def _():
            if t < OWN - 1:
                to_far(t).wait_send()
                forward(t).wait_send()
            else:
                for part in range(4):
                    last_to_far(part).wait_send()

        if t > 0:

            @pl.when(near_ok)
            def _():
                if t < OWN - 1:
                    to_skip(t).wait_send()
                else:
                    for part in range(4):
                        last_to_skip(part).wait_send()


def solution(mesh):
    layers, groups = mesh.shape["layer"], mesh.shape["energy"]

    def local(onsite, broad, ham, coup, mask, prior, weights, offsets):
        n = onsite.shape[-1]
        hbm = pl.BlockSpec(memory_space=pltpu.HBM)
        block = (2 * n, n)
        result = pl.pallas_call(
            functools.partial(kernel, layers, groups),
            out_shape=jax.ShapeDtypeStruct((OWN, 2 * n, n), F32),
            in_specs=[hbm] * 8,
            out_specs=pl.BlockSpec(memory_space=pltpu.VMEM),
            scratch_shapes=[
                pltpu.VMEM((1, n), F32),
                pltpu.VMEM((1, n), F32),
                pltpu.SMEM((TAPS,), F32),
                pltpu.SMEM((TAPS,), jnp.int32),
                pltpu.VMEM((OWN, *block), F32),
                pltpu.VMEM(block, F32),
                pltpu.VMEM(block, F32),
                pltpu.VMEM((n, n), jnp.int32),
                pltpu.VMEM((SLOTS, *block), F32),
                pltpu.VMEM((OWN, *block), F32),
                pltpu.VMEM((OWN, *block), F32),
                pltpu.VMEM(block, F32),
                pltpu.VMEM(block, F32),
                pltpu.VMEM(block, F32),
                pltpu.VMEM(block, F32),
                pltpu.VMEM(block, F32),
                pltpu.VMEM((OWN, *block), F32),
                pltpu.VMEM((20, *block), BF16),
                pltpu.SMEM((SLOTS + 3,), F32),
                pltpu.SemaphoreType.DMA((7,)),
                pltpu.SemaphoreType.DMA((OWN,)),
                pltpu.SemaphoreType.DMA((OWN, 4)),
                pltpu.SemaphoreType.DMA((OWN, 4)),
                pltpu.SemaphoreType.DMA((OWN,)),
                pltpu.SemaphoreType.DMA((OWN,)),
                pltpu.SemaphoreType.DMA((OWN,)),
                pltpu.SemaphoreType.DMA((OWN,)),
                pltpu.SemaphoreType.DMA((SLOTS,)),
                pltpu.SemaphoreType.DMA((2, 4)),
                pltpu.SemaphoreType.DMA((2, 4)),
                pltpu.SemaphoreType.DMA((OWN, 4)),
                pltpu.SemaphoreType.DMA,
                pltpu.SemaphoreType.DMA,
                pltpu.SemaphoreType.DMA,
                pltpu.SemaphoreType.DMA,
                pltpu.SemaphoreType.DMA((OWN,)),
                pltpu.SemaphoreType.DMA((OWN,)),
                pltpu.SemaphoreType.REGULAR,
            ],
            compiler_params=pltpu.CompilerParams(
                collective_id=0, has_side_effects=True, vmem_limit_bytes=50 * 2**20
            ),
        )(
            *(
                pltpu.with_memory_space_constraint(v, pltpu.HBM)
                for v in (
                    onsite,
                    broad,
                    weights,
                    offsets,
                    ham.reshape(block),
                    coup.reshape(block),
                    mask.reshape(n, n),
                    prior.reshape(OWN, *block),
                )
            ),
        )
        return result.reshape(1, OWN, 2, n, n)

    return jax.shard_map(
        local,
        mesh=mesh,
        in_specs=(
            P("layer", None),
            P("layer", None),
            P("layer", None, None, None),
            P("layer", None, None, None),
            P("layer", None, None),
            P("layer", "energy", None, None, None),
            P(),
            P(),
        ),
        out_specs=P("layer", "energy", None, None, None),
        check_vma=False,
    )
```
